128 devices in a mesh: tok: 16 (over x, y), exp: 8 (over z, core).
Axes of the slice: x: 4, y: 4, z: 4, core: 2. Of those that a mesh axis runs over, the one named last changes fastest.
Arguments:
- tokens: bfloat16 [57344, 1536], P('tok'), may hold values from -9 to 9
- dispatch_keys: bfloat16 [512, 1536], P(('tok', 'exp')), may hold values from -0.33458226 to 0.33458226
- expand_weight: bfloat16 [512, 1536, 512], P(('tok', 'exp')), may hold values from -0.15625 to 0.15625
- reduce_weight: bfloat16 [512, 512, 1536], P(('tok', 'exp')), may hold values from -0.25 to 0.25
- teacher: bfloat16 [57344, 1536], P(('tok', 'exp')), may hold values from -9 to 9
Outputs:
- mixed: bfloat16 [57344, 1536], P(('tok', 'exp'))
- loss: float32 [], replicated
- grad_keys: float32 [512, 1536], P(('tok', 'exp'))
The draws below stay inside these ranges and needn't reach their ends.
All inputs are finite; a program needn't handle non-finite values.
Results may differ from the reference program's by a relative error of at most 0.04.
Values may be sent and summed in bfloat16 or wider, within the bound.
A program may use at most 128 MiB of HBM per device.

```python
import math
import jax
import jax.numpy as jnp
from jax import lax

D = 1536
H = 512
SLOTS = 512
TOKENS = 57344


def draw_tokens(key, part):
    key = jax.random.fold_in(key, 1)
    return jax.random.truncated_normal(key, -4.0, 4.0, (TOKENS, D)).astype(jnp.bfloat16)


def draw_dispatch_keys(key, part):
    key = jax.random.fold_in(key, 2)
    spread = 2.5 / math.sqrt(D)
    return (jax.random.truncated_normal(key, -4.0, 4.0, (SLOTS, D)) * spread).astype(jnp.bfloat16)


def draw_teacher(key, part):
    key = jax.random.fold_in(key, 3)
    position = jnp.arange(TOKENS).astype(jnp.float32) / max(TOKENS - 1, 1)
    row_scale = 0.3 * jnp.exp(position * math.log(10.0))
    return (jax.random.truncated_normal(key, -3.0, 3.0, (TOKENS, D)) * row_scale[:, None]).astype(jnp.bfloat16)


def level_of(rng, dims, cuts, low, largest):
    def one(dim, parts):
        steps = jax.random.uniform(jax.random.fold_in(jax.random.fold_in(rng, 6), dim), (parts,), jnp.float32, low / len(cuts), largest / len(cuts))
        return jnp.repeat(jnp.exp(steps), dims[dim] // parts).reshape((-1,) + (1,) * (len(dims) - dim - 1))

    factor_of = one(*cuts[0])
    for cut in cuts[1:]:
        factor_of = factor_of * one(*cut)
    return factor_of


def noise(key, dims, deviation, reach, shards=(), dtype=jnp.bfloat16):
    drawn = deviation * jax.random.normal(key, dims, jnp.float32)
    if shards:
        drawn = drawn * level_of(key, dims, shards, -0.22, 0.18)
    return jnp.clip(drawn, -reach, reach).astype(dtype)


def setup_inputs(seed: int = 0) -> dict:
    splits = jax.random.split(jax.random.key(seed), 6)
    return {
        "tokens": draw_tokens(jax.random.fold_in(splits[5], 71), 0),
        "dispatch_keys": draw_dispatch_keys(jax.random.fold_in(splits[5], 71), 0),
        "expand_weight": noise(splits[2], (SLOTS, D, H), D ** -0.5, 0.15625, ((0, 128),)),
        "reduce_weight": noise(splits[3], (SLOTS, H, D), H ** -0.5, 0.25, ((0, 128),)),
        "teacher": draw_teacher(jax.random.fold_in(splits[5], 71), 0),
    }


gelu_coef = 0.7978845608028654
cube_coef = 0.044715

def gelu_pair(values):
    tanh_value = jnp.tanh(gelu_coef * (values + cube_coef * values * values * values))
    output = 0.5 * values * (1.0 + tanh_value)
    derivative = 0.5 * (1.0 + tanh_value) + 0.5 * values * (1.0 - tanh_value * tanh_value) * gelu_coef * (1.0 + 3.0 * cube_coef * values * values)
    return (output, derivative)

def contract_last(left, right):
    return lax.dot_general(left, right, (((1,), (1,)), ((), ())), preferred_element_type=jnp.float32)

def contract_first(left, right):
    return lax.dot_general(left, right, (((0,), (0,)), ((), ())), preferred_element_type=jnp.float32)

def reference(tokens, dispatch_keys, expand_weight, reduce_weight, teacher):
    highest = lax.Precision.HIGHEST
    logits = contract_last(dispatch_keys, tokens)
    col_max = lax.optimization_barrier(jnp.max(logits, axis=1))
    exp_terms = jnp.exp(logits - col_max[:, None])
    totals = lax.optimization_barrier(jnp.sum(exp_terms, axis=1))
    weights = exp_terms.astype(jnp.bfloat16)
    slot_in = jnp.dot(weights, tokens, preferred_element_type=jnp.float32) / totals[:, None]
    root_mean = jnp.sqrt(lax.optimization_barrier(jnp.mean(slot_in * slot_in, axis=1, keepdims=True)) + 1e-06)
    normed = slot_in / root_mean
    normed_b = normed.astype(jnp.bfloat16)
    pre_act = jnp.einsum('sd,sdh->sh', normed_b.astype(jnp.float32), expand_weight.astype(jnp.float32), precision=highest)
    act_value, gelu_slope = gelu_pair(pre_act)
    activated = act_value.astype(jnp.bfloat16)
    slot_out = jnp.einsum('sh,shd->sd', activated.astype(jnp.float32), reduce_weight.astype(jnp.float32), precision=highest).astype(jnp.bfloat16)
    scores = logits.T
    row_max = lax.optimization_barrier(jnp.max(scores, axis=1, keepdims=True))
    row_terms = jnp.exp(scores - row_max)
    comb = row_terms / lax.optimization_barrier(jnp.sum(row_terms, axis=1, keepdims=True))
    comb_b = comb.astype(jnp.bfloat16)
    result = jnp.dot(comb_b, slot_out, preferred_element_type=jnp.float32)
    mixed = result.astype(jnp.bfloat16)
    misfit = result - teacher.astype(jnp.float32)
    loss = jnp.sum(misfit * misfit) / (2.0 * TOKENS * D)
    grad_rows = (misfit / D).astype(jnp.bfloat16)
    dcomb = contract_last(grad_rows, slot_out)
    dscore = (comb * (dcomb - lax.optimization_barrier(jnp.sum(comb * dcomb, axis=1, keepdims=True)))).astype(jnp.bfloat16)
    key_comb = contract_first(dscore, tokens)
    out_grad = contract_first(comb_b, grad_rows)
    out_grad_b = out_grad.astype(jnp.bfloat16)
    dact = jnp.einsum('sd,shd->sh', out_grad_b.astype(jnp.float32), reduce_weight.astype(jnp.float32), precision=highest)
    dpre = (dact * gelu_slope).astype(jnp.bfloat16)
    dnormed = jnp.einsum('sh,sdh->sd', dpre.astype(jnp.float32), expand_weight.astype(jnp.float32), precision=highest)
    dslot = (dnormed - normed * lax.optimization_barrier(jnp.mean(dnormed * normed, axis=1, keepdims=True))) / root_mean
    scaled_b = (dslot / totals[:, None]).astype(jnp.bfloat16)
    dprob = contract_last(scaled_b, tokens)
    dlogit = (exp_terms * dprob).astype(jnp.bfloat16)
    key_disp = jnp.dot(dlogit, tokens, preferred_element_type=jnp.float32)
    grad_keys = (key_comb + key_disp) / D ** 0.5
    return (mixed, loss, grad_keys)
```

```python
import functools
import jax
import jax.numpy as jnp
from jax import lax
from jax.experimental import pallas as pl
from jax.experimental.pallas import tpu as pltpu
from jax.sharding import PartitionSpec as P

MESH = pl.DeviceIdType.MESH
f32, bf16 = jnp.float32, jnp.bfloat16
D, H, ROWS, PART, OWN, GROUP, HALF = 1536, 512, 3584, 448, 4, 64, 256
Q = 384
EXT = 128
CHUNK = 512
gelu_coef = 0.7978845608028654
cube_coef = 0.044715


def gelu_pair(values):
    tanh_value = jnp.tanh(gelu_coef * (values + cube_coef * values * values * values))
    output = 0.5 * values * (1.0 + tanh_value)
    derivative = 0.5 * (1.0 + tanh_value) + 0.5 * values * (
        1.0 - tanh_value * tanh_value
    ) * gelu_coef * (1.0 + 3.0 * cube_coef * values * values)
    return (output, derivative)


def nn(a, b):
    return lax.dot_general(a, b, (((1,), (0,)), ((), ())), preferred_element_type=f32)


def nt(a, b):
    return lax.dot_general(a, b, (((1,), (1,)), ((), ())), preferred_element_type=f32)


def tn(a, b):
    return lax.dot_general(a, b, (((0,), (0,)), ((), ())), preferred_element_type=f32)


def wait_bytes(ref, sem):
    pltpu.make_async_copy(ref, ref, sem).wait()


def kernel(
    tokens_h, keys, expand_h, reduce_h, teacher_h,
    mixed_h, loss_o, grad_o,
    tokens, expand, reduce_, teacher,
    perm, perm_t, stack, wide,
    own_msg, gath_k, all_keys, group_keys,
    terms, weights, partial, msg_b, recv_b,
    normed, x16, out_msg, gath_o, every_out,
    comb, comb_b, grad_rows, mixed,
    half, cross_send, cross_recv, msg_d, recv_d,
    cross_send2, cross_recv2, msg_e, recv_e, loss_own, loss_other,
    f_msg, recv_f, msg_g, recv_g,
    load_sem, mixed_sem, send_k, recv_k, csend_k, crecv_k, send_b, rsem_b,
    send_o, recv_o, csend_o, crecv_o, csend_d, crecv_d, send_d, rsem_d,
    csend_e, crecv_e, send_e, rsem_e, csend_l, crecv_l,
    send_f, rsem_f, send_g, rsem_g,
):
    t = lax.axis_index("tok")
    e = lax.axis_index("exp")
    x, y = lax.div(t, 4), lax.rem(t, 4)
    z, c = lax.div(e, 2), lax.rem(e, 2)
    other = (t, z * 2 + 1 - c)

    loads = [
        pltpu.make_async_copy(tokens_h, tokens, load_sem.at[0]),
        pltpu.make_async_copy(expand_h, expand, load_sem.at[1]),
        pltpu.make_async_copy(reduce_h, reduce_, load_sem.at[2]),
        pltpu.make_async_copy(teacher_h, teacher, load_sem.at[3]),
    ]
    for load in loads:
        load.start()

    def peer(k):
        kt = lax.rem(k, 16)
        x2 = lax.rem(x + lax.div(kt, 4), 4)
        y2 = lax.rem(y + lax.rem(kt, 4), 4)
        z2 = lax.rem(z + lax.div(k, 16), 4)
        return x2 * 4 + y2, z2

    barrier = pltpu.get_barrier_semaphore()

    def greet(k, carry):
        t2, z2 = peer(k)
        pl.semaphore_signal(barrier, inc=1, device_id=(t2, z2 * 2 + c), device_id_type=MESH)
        return carry

    lax.fori_loop(1, 64, greet, 0)
    pl.semaphore_signal(barrier, inc=1, device_id=other, device_id_type=MESH)

    row = lax.broadcasted_iota(jnp.int32, (256, 256), 0)
    col = lax.broadcasted_iota(jnp.int32, (256, 256), 1)

    def moved(r):
        return ((r >> 2) & 15) * 16 + (r >> 6) * 4 + (r & 3)

    perm[...] = jnp.where(col == moved(row), 1.0, 0.0).astype(bf16)
    perm_t[...] = jnp.where(row == moved(col), 1.0, 0.0).astype(bf16)

    def pack(value):
        for j in range(4):
            wide[4 * j : 4 * j + 4, :Q] = value[0:4, Q * j : Q * j + Q]
        return wide[:, :Q]

    def unpack(message):
        wide[:, :Q] = message
        x16[...] = jnp.zeros((16, D), f32)
        for j in range(4):
            x16[0:4, Q * j : Q * j + Q] = wide[4 * j : 4 * j + 4, :Q]

    def spread(rows_, width):
        return nn(perm_t[...], stack[:, :width]).astype(bf16).reshape(16, 16, width)

    def to_stack(value):
        for j in range(4):
            stack[64 * j : 64 * j + 64, :Q] = value[:, Q * j : Q * j + Q].astype(bf16)

    def settle(block, dst, at):
        r = nn(perm[...], block).astype(bf16)
        for j in range(4):
            dst[pl.ds(at, 64), Q * j : Q * j + Q] = r[64 * j : 64 * j + 64]

    def gather_start(src, gath, send, recv):
        pltpu.make_async_copy(src, gath.at[0, z * 16 + t], recv.at[z]).start()

        def step(k, carry):
            t2, z2 = peer(k)
            pltpu.make_async_remote_copy(
                src, gath.at[0, z * 16 + t], send, recv.at[z],
                device_id=(t2, z2 * 2 + c), device_id_type=MESH,
            ).start()
            return carry

        lax.fori_loop(1, 64, step, 0)

    def gather_pass(gath, recv, csend, crecv, dz):
        zz = lax.rem(z + dz, 4)
        part = gath.at[0, pl.ds(zz * 16, 16)]
        wait_bytes(part, recv.at[zz])
        pltpu.make_async_remote_copy(
            part, gath.at[1, pl.ds(zz * 16, 16)], csend.at[zz], crecv.at[zz],
            device_id=other, device_id_type=MESH,
        ).start()
        return zz

    def gather_settle(gath, half_, zz, dst):
        block = gath[half_, pl.ds(zz * 16, 16)].reshape(256, Q)
        settle(block, dst, pl.multiple_of(half_ * 256 + zz * 64, 64))

    def gather_end(gath, send, csend):
        wait_bytes(gath.at[0, pl.ds(0, 63)], send)
        for k in range(4):
            wait_bytes(gath.at[0, pl.ds(0, 16)], csend.at[k])

    def tok_start(src_of, recv_ref, send, recv):
        pltpu.make_async_copy(src_of(t), recv_ref.at[t], recv).start()

        def step(k, carry):
            t2, _ = peer(k)
            pltpu.make_async_remote_copy(
                src_of(t2), recv_ref.at[t], send, recv,
                device_id=(t2, e), device_id_type=MESH,
            ).start()
            return carry

        lax.fori_loop(1, 16, step, 0)

    def all_start(msg, recv_ref, send, recv):
        me = z * 16 + t
        pltpu.make_async_copy(msg.at[me], recv_ref.at[me], recv).start()

        def step(k, carry):
            t2, z2 = peer(k)
            pltpu.make_async_remote_copy(
                msg.at[z2 * 16 + t2], recv_ref.at[me], send, recv,
                device_id=(t2, z2 * 2 + c), device_id_type=MESH,
            ).start()
            return carry

        lax.fori_loop(1, 64, step, 0)

    def gather_sum(ref, n):
        return lax.fori_loop(
            0, n, lambda k, s: s + ref[k].astype(f32), jnp.zeros(ref.shape[1:], f32)
        )

    own_msg[...] = pack(keys[...].astype(f32)).astype(bf16)
    pl.semaphore_wait(barrier, 64)

    gather_start(own_msg, gath_k, send_k, recv_k)
    gather_pass(gath_k, recv_k, csend_k, crecv_k, 0)
    settle(gath_k[0, pl.ds(z * 16, 16)].reshape(256, Q), group_keys, 0)
    loads[0].wait()

    @pl.loop(0, ROWS // CHUNK)
    def _(n):
        at = pl.multiple_of(n * CHUNK, CHUNK)
        terms[:, pl.ds(at, CHUNK)] = nt(group_keys[...], tokens[pl.ds(at, CHUNK), :])

    top = jnp.max(terms[...], axis=1, keepdims=True).astype(bf16).astype(f32)
    exp_terms = jnp.exp(terms[...] - top)
    terms[...] = exp_terms
    weights[...] = exp_terms.astype(bf16)
    total = jnp.sum(exp_terms, axis=1, keepdims=True)

    def column_pass():
        @pl.loop(0, D // 256)
        def _(n):
            at = pl.multiple_of(n * 256, 256)
            partial[:, pl.ds(at, 256)] = nn(weights[...], tokens[:, pl.ds(at, 256)])

    column_pass()
    to_stack(partial[...])
    lane = lax.broadcasted_iota(jnp.int32, (64, EXT), 1)
    total_hi = total.astype(bf16).astype(f32)
    extra = jnp.where(lane == 0, top, jnp.where(lane == 1, total_hi, jnp.where(lane == 2, total - total_hi, 0.0)))
    for j in range(4):
        stack[64 * j : 64 * j + 64, Q:] = extra.astype(bf16)
    msg_b[...] = spread(stack, Q + EXT)
    tok_start(lambda k: msg_b.at[k], recv_b, send_b, rsem_b)

    for dz in range(1, 4):
        gather_pass(gath_k, recv_k, csend_k, crecv_k, dz)
    for k in range(4):
        gather_settle(gath_k, 0, k, all_keys)
    for k in range(4):
        wait_bytes(gath_k.at[1, pl.ds(k * 16, 16)], crecv_k.at[k])
        gather_settle(gath_k, 1, k, all_keys)
    local = tokens.at[pl.ds(pl.multiple_of(e * PART, 64), PART)]
    scores = nt(local[...], all_keys[...])
    row_terms = jnp.exp(scores - jnp.max(scores, axis=1, keepdims=True))
    comb_v = row_terms / jnp.sum(row_terms, axis=1, keepdims=True)
    comb[...] = comb_v
    comb_b[...] = comb_v.astype(bf16)

    wait_bytes(recv_b, rsem_b)
    best = recv_b[0, :, Q : Q + 1].astype(f32)
    for k in range(1, 16):
        best = jnp.maximum(best, recv_b[k, :, Q : Q + 1].astype(f32))
    slot_sum = jnp.zeros((16, Q), f32)
    slot_total = jnp.zeros((16, 1), f32)
    for k in range(16):
        scale = jnp.exp(recv_b[k, :, Q : Q + 1].astype(f32) - best)
        slot_sum += scale * recv_b[k, :, :Q].astype(f32)
        slot_total += scale * (
            recv_b[k, :, Q + 1 : Q + 2].astype(f32) + recv_b[k, :, Q + 2 : Q + 3].astype(f32)
        )
    unpack(slot_sum / slot_total)
    slot_in = x16[...]
    root_mean = jnp.sqrt(jnp.mean(slot_in * slot_in, axis=1, keepdims=True) + 1e-06)
    normed_v = slot_in / root_mean
    normed[...] = normed_v
    normed_b = normed_v.astype(bf16)

    loads[1].wait()
    loads[2].wait()
    row_h = lax.broadcasted_iota(jnp.int32, (16, H), 0)
    row_d = lax.broadcasted_iota(jnp.int32, (16, D), 0)
    pre_act = jnp.zeros((16, H), f32)
    for s in range(OWN):
        pre_act = jnp.where(row_h == s, nn(normed_b, expand[s]), pre_act)
    act_value, gelu_slope = gelu_pair(pre_act)
    act_b = act_value.astype(bf16)
    slot_out = jnp.zeros((16, D), f32)
    for s in range(OWN):
        slot_out = jnp.where(row_d == s, nn(act_b, reduce_[s]), slot_out)
    out_msg[...] = pack(slot_out).astype(bf16)

    gather_start(out_msg, gath_o, send_o, recv_o)
    for dz in range(4):
        zz = gather_pass(gath_o, recv_o, csend_o, crecv_o, dz)
        gather_settle(gath_o, 0, zz, every_out)
    for k in range(4):
        wait_bytes(gath_o.at[1, pl.ds(k * 16, 16)], crecv_o.at[k])
        gather_settle(gath_o, 1, k, every_out)

    loads[3].wait()
    loss_own[...] = jnp.zeros((8, 128), f32)
    for n in range(2):
        cols = slice(768 * n, 768 * n + 768)
        result = nn(comb_b[...], every_out[:, cols])
        mixed[:, cols] = result.astype(bf16)
        misfit = result - teacher[:, cols].astype(f32)
        loss_own[...] += jnp.sum(misfit * misfit)
        grad_v = (misfit / D).astype(bf16)
        grad_rows[:, cols] = grad_v
        out_part = tn(comb_b[...], grad_v)
        half[:, cols] = out_part[:HALF]
        cross_send[n] = out_part[HALF:].astype(bf16)
        pltpu.make_async_remote_copy(
            cross_send.at[n], cross_recv.at[n], csend_d.at[n], crecv_d.at[n],
            device_id=other, device_id_type=MESH,
        ).start()
    mixed_copy = pltpu.make_async_copy(mixed, mixed_h, mixed_sem)
    mixed_copy.start()
    loss_copy = pltpu.make_async_remote_copy(
        loss_own, loss_other, csend_l, crecv_l, device_id=other, device_id_type=MESH
    )
    loss_copy.start()

    def fold(cross, sem):
        for n in range(2):
            wait_bytes(cross.at[n], sem.at[n])
            cols = slice(768 * n, 768 * n + 768)
            half[:, cols] += cross[n].astype(f32)

    fold(cross_recv, crecv_d)
    for k in range(4):
        to_stack(half[64 * k : 64 * k + 64, :])
        msg_d[16 * k : 16 * k + 16] = spread(stack, Q)
    all_start(msg_d, recv_d, send_d, rsem_d)

    dcomb = nt(grad_rows[...], every_out[...])
    weighted_d = comb[...] * dcomb
    dscore = (weighted_d - comb[...] * jnp.sum(weighted_d, axis=1, keepdims=True)).astype(bf16)
    for n in range(2):
        cols = slice(768 * n, 768 * n + 768)
        key_part = tn(dscore, local[:, cols])
        half[:, cols] = key_part[:HALF]
        cross_send2[n] = key_part[HALF:].astype(bf16)
        pltpu.make_async_remote_copy(
            cross_send2.at[n], cross_recv2.at[n], csend_e.at[n], crecv_e.at[n],
            device_id=other, device_id_type=MESH,
        ).start()
    fold(cross_recv2, crecv_e)
    loss_copy.wait()
    chip_loss = loss_own[0:1, 0:1] + loss_other[0:1, 0:1]
    loss_hi = chip_loss.astype(bf16).astype(f32)
    loss_mid = (chip_loss - loss_hi).astype(bf16).astype(f32)
    extra_l = jnp.where(
        lane == 0, loss_hi, jnp.where(lane == 1, loss_mid, jnp.where(lane == 2, chip_loss - loss_hi - loss_mid, 0.0))
    )
    for j in range(4):
        stack[64 * j : 64 * j + 64, Q:] = extra_l.astype(bf16)
    for k in range(4):
        to_stack(half[64 * k : 64 * k + 64, :])
        msg_e[16 * k : 16 * k + 16] = spread(stack, Q + EXT)
    all_start(msg_e, recv_e, send_e, rsem_e)

    wait_bytes(recv_d, rsem_d)
    unpack(gather_sum(recv_d, 64))
    out_grad = x16[...].astype(bf16)
    dact = jnp.zeros((16, H), f32)
    for s in range(OWN):
        dact = jnp.where(row_h == s, nt(out_grad, reduce_[s]), dact)
    dpre = (dact * gelu_slope).astype(bf16)
    dnormed = jnp.zeros((16, D), f32)
    for s in range(OWN):
        dnormed = jnp.where(row_d == s, nt(dpre, expand[s]), dnormed)
    normed_v = normed[...]
    dslot = (dnormed - normed_v * jnp.mean(dnormed * normed_v, axis=1, keepdims=True)) / root_mean
    f_msg[:, :Q] = (pack(dslot) / slot_total).astype(bf16)
    f_msg[:, Q:] = jnp.broadcast_to(best, (16, EXT)).astype(bf16)
    tok_start(lambda k: f_msg, recv_f, send_f, rsem_f)

    wait_bytes(recv_f, rsem_f)
    back = nn(perm[...], recv_f[...].reshape(256, Q + EXT))
    for j in range(4):
        group_keys[:, Q * j : Q * j + Q] = back[64 * j : 64 * j + 64, :Q].astype(bf16)
    factor = jnp.exp(top - back[0:64, Q : Q + 1])

    @pl.loop(0, ROWS // CHUNK)
    def _(n):
        at = pl.multiple_of(n * CHUNK, CHUNK)
        dprob = nt(group_keys[...], tokens[pl.ds(at, CHUNK), :])
        weights[:, pl.ds(at, CHUNK)] = (terms[:, pl.ds(at, CHUNK)] * factor * dprob).astype(bf16)

    column_pass()
    to_stack(partial[...])
    msg_g[...] = spread(stack, Q)
    tok_start(lambda k: msg_g.at[k], recv_g, send_g, rsem_g)

    wait_bytes(recv_e, rsem_e)
    key_comb = gather_sum(recv_e, 64)
    loss_total = key_comb[0:1, Q : Q + 1] + key_comb[0:1, Q + 1 : Q + 2] + key_comb[0:1, Q + 2 : Q + 3]
    loss_o[...] = jnp.broadcast_to(loss_total / (2.0 * 16 * ROWS * D), (8, 128))
    wait_bytes(recv_g, rsem_g)
    key_disp = gather_sum(recv_g, 16)
    unpack((key_comb[:, :Q] + key_disp) / D**0.5)
    grad_o[...] = x16[0:4, :]

    gather_end(gath_k, send_k, csend_k)
    gather_end(gath_o, send_o, csend_o)
    wait_bytes(msg_b.at[pl.ds(0, 15)], send_b)
    wait_bytes(recv_f.at[pl.ds(0, 15)], send_f)
    wait_bytes(msg_g.at[pl.ds(0, 15)], send_g)
    wait_bytes(msg_d.at[pl.ds(0, 63)], send_d)
    wait_bytes(msg_e.at[pl.ds(0, 63)], send_e)
    for n in range(2):
        wait_bytes(cross_send.at[n], csend_d.at[n])
        wait_bytes(cross_send2.at[n], csend_e.at[n])
    mixed_copy.wait()


def body(tokens, dispatch_keys, expand_weight, reduce_weight, teacher):
    any_spec = pl.BlockSpec(memory_space=pl.ANY)
    vmem_spec = pl.BlockSpec(memory_space=pltpu.VMEM)
    V = pltpu.VMEM
    dma = pltpu.SemaphoreType.DMA
    mixed, loss, grad = pl.pallas_call(
        kernel,
        out_shape=(
            jax.ShapeDtypeStruct((PART, D), bf16),
            jax.ShapeDtypeStruct((8, 128), f32),
            jax.ShapeDtypeStruct((OWN, D), f32),
        ),
        in_specs=[any_spec, vmem_spec, any_spec, any_spec, any_spec],
        out_specs=(any_spec, vmem_spec, vmem_spec),
        scratch_shapes=[
            V((ROWS, D), bf16), V((OWN, D, H), bf16), V((OWN, H, D), bf16), V((PART, D), bf16),
            V((256, 256), bf16), V((256, 256), bf16), V((256, Q + EXT), bf16), V((16, Q + EXT), f32),
            V((16, Q), bf16), V((2, 64, 16, Q), bf16), V((512, D), bf16), V((64, D), bf16),
            V((64, ROWS), f32), V((64, ROWS), bf16), V((64, D), f32), V((16, 16, Q + EXT), bf16), V((16, 16, Q + EXT), bf16),
            V((16, D), f32), V((16, D), f32), V((16, Q), bf16), V((2, 64, 16, Q), bf16), V((512, D), bf16),
            V((PART, 512), f32), V((PART, 512), bf16), V((PART, D), bf16), V((PART, D), bf16),
            V((HALF, D), f32), V((2, HALF, 768), bf16), V((2, HALF, 768), bf16), V((64, 16, Q), bf16), V((64, 16, Q), bf16),
            V((2, HALF, 768), bf16), V((2, HALF, 768), bf16), V((64, 16, Q + EXT), bf16), V((64, 16, Q + EXT), bf16),
            V((8, 128), f32), V((8, 128), f32),
            V((16, Q + EXT), bf16), V((16, 16, Q + EXT), bf16), V((16, 16, Q), bf16), V((16, 16, Q), bf16),
            dma((4,)), dma, dma, dma((4,)), dma((4,)), dma((4,)), dma, dma,
            dma, dma((4,)), dma((4,)), dma((4,)), dma((2,)), dma((2,)), dma, dma,
            dma((2,)), dma((2,)), dma, dma, dma, dma,
            dma, dma, dma, dma,
        ],
        compiler_params=pltpu.CompilerParams(
            collective_id=0, has_side_effects=True, vmem_limit_bytes=60 * 2**20
        ),
    )(tokens, dispatch_keys, expand_weight, reduce_weight, teacher)
    return mixed, loss[0, 0], grad


def solution(mesh):
    in_specs = (
        P("tok", None),
        P(("tok", "exp"), None),
        P(("tok", "exp"), None, None),
        P(("tok", "exp"), None, None),
        P(("tok", "exp"), None),
    )
    out_specs = (P(("tok", "exp"), None), P(), P(("tok", "exp"), None))
    return jax.shard_map(body, mesh=mesh, in_specs=in_specs, out_specs=out_specs, check_vma=False)
```

```python
import functools
import jax
import jax.numpy as jnp
from jax import lax
from jax.experimental import pallas as pl
from jax.experimental.pallas import tpu as pltpu
from jax.sharding import PartitionSpec as P

MESH = pl.DeviceIdType.MESH
f32, bf16 = jnp.float32, jnp.bfloat16
D, H, ROWS, PART, OWN, GROUP, HALF = 1536, 512, 3584, 448, 4, 64, 256
TOK = 16
PARTS = 3
WIDE = 512
LANES = 128
Q = PARTS * LANES
CHUNK = 1792
gelu_coef = 0.7978845608028654
cube_coef = 0.044715


def gelu_pair(values):
    tanh_value = jnp.tanh(gelu_coef * (values + cube_coef * values * values * values))
    output = 0.5 * values * (1.0 + tanh_value)
    derivative = 0.5 * (1.0 + tanh_value) + 0.5 * values * (
        1.0 - tanh_value * tanh_value
    ) * gelu_coef * (1.0 + 3.0 * cube_coef * values * values)
    return (output, derivative)


def nn(a, b):
    return lax.dot_general(a, b, (((1,), (0,)), ((), ())), preferred_element_type=f32)


def nt(a, b):
    return lax.dot_general(a, b, (((1,), (1,)), ((), ())), preferred_element_type=f32)


def tn(a, b):
    return lax.dot_general(a, b, (((0,), (0,)), ((), ())), preferred_element_type=f32)


def wait_bytes(ref, sem):
    pltpu.make_async_copy(ref, ref, sem).wait()


class Pending:
    def __init__(self):
        self.open = {}

    def add(self, name, ref, sem):
        self.open[name] = (ref, sem)

    def wait(self, name):
        wait_bytes(*self.open.pop(name))

    def finish(self):
        for name in list(self.open):
            self.wait(name)


def kernel(
    tokens_h, keys, expand_h, reduce_h, teacher_h,
    mixed_h, loss_o, grad_o,
    tokens, expand, reduce_, teacher, perm, perm_t, wide,
    key_msg, recv_k, all_keys,
    terms, weights, msg_b, recv_b,
    normed, x16, out_msg, gath_o, every_out,
    comb, comb_b, grad_rows, mixed,
    half_d, cross_d, arrived_d, msg_d, recv_d,
    half_e, cross_e, arrived_e, fold_e, recv_e, loss_own, loss_other, loss_z,
    msg_f, recv_f, msg_g, recv_g,
    load_sem, mixed_sem, ssem_k, rsem_k, ssem_kz, rsem_kz, csend_k, crecv_k,
    ssem_b, rsem_b, ssem_o, rsem_o, csend_o, crecv_o,
    csend_d, crecv_d, ssem_d, rsem_d, csend_e, crecv_e, ssem_e, rsem_e,
    csend_l, crecv_l, ssem_l, rsem_l, ssem_f, rsem_f, ssem_g, rsem_g,
):
    t = lax.axis_index("tok")
    e = lax.axis_index("exp")
    x, y = t >> 2, t & 3
    z, c = e >> 1, e & 1
    other = (t, z * 2 + 1 - c)
    flying = Pending()
    finish = flying.finish

    for n, (name, src, dst) in enumerate((
        ("tokens", tokens_h, tokens), ("expand", expand_h, expand),
        ("reduce", reduce_h, reduce_), ("teacher", teacher_h, teacher),
    )):
        pltpu.make_async_copy(src, dst, load_sem.at[n]).start()
        flying.add(name, dst, load_sem.at[n])

    def peer(k):
        t2 = ((x + ((k >> 2) & 3)) & 3) * 4 + ((y + (k & 3)) & 3)
        return t2, (z + (k >> 4)) & 3

    barrier = pltpu.get_barrier_semaphore()

    def greet(k, carry):
        t2, z2 = peer(k)
        pl.semaphore_signal(barrier, inc=1, device_id=(t2, z2 * 2 + c), device_id_type=MESH)
        return carry

    lax.fori_loop(1, 64, greet, 0)
    pl.semaphore_signal(barrier, inc=1, device_id=other, device_id_type=MESH)

    row = lax.broadcasted_iota(jnp.int32, (256, 256), 0)
    col = lax.broadcasted_iota(jnp.int32, (256, 256), 1)

    def moved(r):
        return ((r >> 2) & 15) * 16 + (r >> 6) * 4 + (r & 3)

    perm[...] = jnp.where(col == moved(row), 1.0, 0.0).astype(bf16)
    perm_t[...] = jnp.where(row == moved(col), 1.0, 0.0).astype(bf16)

    def place(n, j):
        return slice(WIDE * n + LANES * j, WIDE * n + LANES * j + LANES)

    def span(n, width=LANES):
        return slice(width * n, width * n + width)

    def pack(value):
        for n in range(PARTS):
            for j in range(4):
                wide[4 * j : 4 * j + 4, span(n)] = value[0:4, place(n, j)]
        return wide[...]

    def unpack(message, n):
        wide[:, span(n)] = message
        for j in range(4):
            x16[0:4, place(n, j)] = wide[4 * j : 4 * j + 4, span(n)]

    def lines(value):
        return jnp.concatenate([value[:, span(j)] for j in range(4)], axis=0).astype(bf16)

    def spread(stacked):
        return nn(perm_t[...], stacked).astype(bf16)

    def remote(src, dst, send, recv, device):
        pltpu.make_async_remote_copy(
            src, dst, send, recv, device_id=device, device_id_type=MESH
        ).start()

    def cross(name, src, dst, send, recv):
        remote(src, dst, send, recv, other)
        flying.add(name + "_out", src, send)
        flying.add(name + "_in", dst, recv)

    def to_tok(name, src_of, recv_ref, send, recv):
        pltpu.make_async_copy(src_of(t), recv_ref.at[t], recv).start()

        def step(k, carry):
            t2, _ = peer(k)
            remote(src_of(t2), recv_ref.at[t], send, recv, (t2, e))
            return carry

        lax.fori_loop(1, TOK, step, 0)
        flying.add(name + "_out", recv_ref.at[pl.ds(0, TOK - 1)], send)
        flying.add(name + "_in", recv_ref, recv)

    def to_all(name, src_of, recv_ref, send, recv):
        me = z * TOK + t
        pltpu.make_async_copy(src_of(me), recv_ref.at[me], recv).start()

        def step(k, carry):
            t2, z2 = peer(k)
            remote(src_of(z2 * TOK + t2), recv_ref.at[me], send, recv, (t2, z2 * 2 + c))
            return carry

        lax.fori_loop(1, 64, step, 0)
        flying.add(name + "_out", recv_ref.at[pl.ds(0, 63)], send)
        flying.add(name + "_in", recv_ref, recv)

    def to_z(name, src_of, dst, send, recv, three):
        for dz in range(1, 4):
            z2 = (z + dz) & 3
            remote(src_of(z2), dst, send, recv, (t, z2 * 2 + c))
        flying.add(name + "_out", three, send)

    def sum_of(ref, count):
        return lax.fori_loop(
            0, count, lambda k, s: s + ref[k].astype(f32), jnp.zeros(ref.shape[1:], f32)
        )

    x16[...] = jnp.zeros((16, D), f32)
    key_msg[...] = pack(keys[...].astype(f32)).astype(bf16)
    pl.semaphore_wait(barrier, 64)

    to_tok("keys", lambda k: key_msg, recv_k, ssem_k, rsem_k)
    flying.wait("keys_in")
    mine = pl.ds(pl.multiple_of(z * GROUP, GROUP), GROUP)
    moved_k = nn(perm[...], recv_k[...].reshape(256, Q)).astype(bf16)
    for n in range(PARTS):
        for j in range(4):
            all_keys[mine, place(n, j)] = moved_k[64 * j : 64 * j + 64, span(n)]

    def key_rows(half, dz):
        return pl.ds(pl.multiple_of(half * HALF + ((z + dz) & 3) * GROUP, GROUP), GROUP)

    def key_cross(dz):
        zz = (z + dz) & 3
        cross(
            f"keys_cross{dz}", all_keys.at[key_rows(0, dz)], all_keys.at[key_rows(1, dz)],
            csend_k.at[zz], crecv_k.at[zz],
        )

    to_z(
        "keys_z", lambda z2: all_keys.at[mine], all_keys.at[mine], ssem_kz, rsem_kz.at[z],
        all_keys.at[pl.ds(0, 3 * GROUP)],
    )
    for dz in range(1, 4):
        flying.add(f"keys_z{dz}", all_keys.at[key_rows(0, dz)], rsem_kz.at[(z + dz) & 3])
    key_cross(0)
    flying.wait("tokens")

    @pl.loop(0, ROWS // CHUNK)
    def _(n):
        at = pl.multiple_of(n * CHUNK, CHUNK)
        terms[:, pl.ds(at, CHUNK)] = nt(all_keys[mine, :], tokens[pl.ds(at, CHUNK), :])

    top = jnp.max(terms[...], axis=1, keepdims=True).astype(bf16).astype(f32)
    exp_terms = jnp.exp(terms[...] - top)
    terms[...] = exp_terms
    weights[...] = exp_terms.astype(bf16)
    total = jnp.sum(exp_terms, axis=1, keepdims=True)
    lane = lax.broadcasted_iota(jnp.int32, (GROUP, LANES), 1)
    total_hi = total.astype(bf16).astype(f32)
    extra = jnp.where(
        lane == 0, top, jnp.where(lane == 1, total_hi, jnp.where(lane == 2, total - total_hi, 0.0))
    )
    extra_b = extra.astype(bf16)
    msg_b[PARTS] = spread(jnp.concatenate([extra_b] * 4, axis=0)).reshape(TOK, 16, LANES)
    to_tok("b3", lambda k: msg_b.at[PARTS, k], recv_b.at[PARTS], ssem_b.at[PARTS], rsem_b.at[PARTS])
    for n in range(PARTS):
        part = nn(weights[...], tokens[:, span(n, WIDE)])
        msg_b[n] = spread(lines(part)).reshape(TOK, 16, LANES)
        to_tok(f"b{n}", lambda k: msg_b.at[n, k], recv_b.at[n], ssem_b.at[n], rsem_b.at[n])

    for dz in range(1, 4):
        flying.wait(f"keys_z{dz}")
        key_cross(dz)
    for dz in range(4):
        flying.wait(f"keys_cross{dz}_in")
    local = tokens.at[pl.ds(pl.multiple_of(e * PART, GROUP), PART)]
    scores = nt(local[...], all_keys[...])
    row_terms = jnp.exp(scores - jnp.max(scores, axis=1, keepdims=True))
    comb_v = row_terms / jnp.sum(row_terms, axis=1, keepdims=True)
    comb[...] = comb_v
    comb_b[...] = comb_v.astype(bf16)

    flying.wait("b3_in")
    best = recv_b[PARTS, 0, :, 0:1].astype(f32)
    for k in range(1, TOK):
        best = jnp.maximum(best, recv_b[PARTS, k, :, 0:1].astype(f32))
    scales = []
    slot_total = jnp.zeros((16, 1), f32)
    for k in range(TOK):
        held = recv_b[PARTS, k].astype(f32)
        scales.append(jnp.exp(held[:, 0:1] - best))
        slot_total += scales[k] * (held[:, 1:2] + held[:, 2:3])
    for n in range(PARTS):
        flying.wait(f"b{n}_in")
        slot_sum = jnp.zeros((16, LANES), f32)
        for k in range(TOK):
            slot_sum += scales[k] * recv_b[n, k].astype(f32)
        unpack(slot_sum / slot_total, n)
    slot_in = x16[...]
    root_mean = jnp.sqrt(jnp.mean(slot_in * slot_in, axis=1, keepdims=True) + 1e-06)
    normed_v = slot_in / root_mean
    normed[...] = normed_v
    normed_b = normed_v.astype(bf16)

    flying.wait("expand")
    flying.wait("reduce")
    row_h = lax.broadcasted_iota(jnp.int32, (16, H), 0)
    row_d = lax.broadcasted_iota(jnp.int32, (16, D), 0)
    pre_act = jnp.zeros((16, H), f32)
    for s in range(OWN):
        pre_act = jnp.where(row_h == s, nn(normed_b, expand[s]), pre_act)
    act_value, gelu_slope = gelu_pair(pre_act)
    act_b = act_value.astype(bf16)
    slot_out = jnp.zeros((16, D), f32)
    for s in range(OWN):
        slot_out = jnp.where(row_d == s, nn(act_b, reduce_[s]), slot_out)
    packed_out = pack(slot_out).astype(bf16)
    for n in range(PARTS):
        out_msg[n] = packed_out[:, span(n)]
    for n in range(PARTS):
        to_all(f"o{n}", lambda k: out_msg.at[n], gath_o.at[n, 0], ssem_o.at[n], rsem_o.at[n])

    flying.wait("teacher")

    def settle(n, half):
        block = jnp.concatenate(
            [gath_o[n, half, span(g, TOK)].reshape(256, LANES) for g in range(4)], axis=1
        )
        r = nn(perm[...], block).astype(bf16)
        for g in range(4):
            for j in range(4):
                every_out[half * HALF + g * GROUP : half * HALF + (g + 1) * GROUP, place(n, j)] = r[
                    64 * j : 64 * j + 64, span(g)
                ]

    def pass_on(n):
        flying.wait(f"o{n}_in")
        cross(f"o_cross{n}", gath_o.at[n, 0], gath_o.at[n, 1], csend_o.at[n], crecv_o.at[n])
        settle(n, 0)

    def combine(n):
        flying.wait(f"o_cross{n}_in")
        settle(n, 1)
        cols = span(n, WIDE)
        result = nn(comb_b[...], every_out[:, cols])
        mixed[:, cols] = result.astype(bf16)
        misfit = result - teacher[:, cols].astype(f32)
        grad_v = (misfit / D).astype(bf16)
        grad_rows[:, cols] = grad_v
        out_part = tn(comb_b[...], grad_v)
        half_d[:, cols] = out_part[:HALF]
        cross_d[n] = out_part[HALF:].astype(bf16)
        cross(f"d_cross{n}", cross_d.at[n], arrived_d.at[n], csend_d.at[n], crecv_d.at[n])
        return jnp.sum(misfit * misfit)

    def send_d(n):
        flying.wait(f"d_cross{n}_in")
        whole = half_d[:, span(n, WIDE)] + arrived_d[n].astype(f32)
        stacked = jnp.concatenate([lines(whole[span(g, GROUP)]) for g in range(4)], axis=1)
        r = spread(stacked)
        for g in range(4):
            msg_d[n, span(g, TOK)] = r[:, span(g)].reshape(TOK, 16, LANES)
        to_all(f"d{n}", lambda k: msg_d.at[n, k], recv_d.at[n], ssem_d.at[n], rsem_d.at[n])

    pass_on(0)
    loss_sum = combine(0)
    pass_on(1)
    send_d(0)
    loss_sum += combine(1)
    pass_on(2)
    send_d(1)
    loss_sum += combine(2)
    loss_own[...] = jnp.full((8, LANES), loss_sum, f32)
    cross("loss", loss_own, loss_other, csend_l, crecv_l)
    send_d(2)
    pltpu.make_async_copy(mixed, mixed_h, mixed_sem).start()
    flying.add("mixed", mixed, mixed_sem)

    dcomb = nt(grad_rows[...], every_out[...])
    weighted_d = comb[...] * dcomb
    dscore = (weighted_d - comb[...] * jnp.sum(weighted_d, axis=1, keepdims=True)).astype(bf16)
    for n in range(PARTS):
        key_part = tn(dscore, local[:, span(n, WIDE)])
        half_e[:, span(n, WIDE)] = key_part[:HALF]
        cross_e[n] = key_part[HALF:].astype(bf16)
        cross(f"e_cross{n}", cross_e.at[n], arrived_e.at[n], csend_e.at[n], crecv_e.at[n])
    flying.wait("loss_in")
    loss_z[z] = loss_own[...] + loss_other[...]
    to_z("loss_z", lambda z2: loss_z.at[z], loss_z.at[z], ssem_l, rsem_l.at[z], loss_z.at[pl.ds(0, 3)])
    for dz in range(1, 4):
        flying.add(f"loss_z{dz}", loss_z.at[(z + dz) & 3], rsem_l.at[(z + dz) & 3])
    for n in range(PARTS):
        flying.wait(f"e_cross{n}_in")
        whole_e = (half_e[:, span(n, WIDE)] + arrived_e[n].astype(f32)).astype(bf16)
        for g in range(4):
            fold_e[g, :, span(n, WIDE)] = whole_e[span(g, GROUP)]

    dact = jnp.zeros((16, H), f32)
    for n in range(PARTS):
        flying.wait(f"d{n}_in")
        unpack(sum_of(recv_d.at[n], 64), n)
        cols = span(n, WIDE)
        out_grad = x16[:, cols].astype(bf16)
        for s in range(OWN):
            dact = jnp.where(row_h == s, dact + nt(out_grad, reduce_[s, :, cols]), dact)
    to_z("e", lambda z2: fold_e.at[z2], recv_e.at[z], ssem_e, rsem_e, fold_e.at[pl.ds(0, 3)])
    pltpu.make_async_copy(fold_e.at[z], recv_e.at[z], rsem_e).start()
    flying.add("e_in", recv_e, rsem_e)
    dpre = (dact * gelu_slope).astype(bf16)
    dnormed = jnp.zeros((16, D), f32)
    for s in range(OWN):
        dnormed = jnp.where(row_d == s, nt(dpre, expand[s]), dnormed)
    normed_v = normed[...]
    dslot = (dnormed - normed_v * jnp.mean(dnormed * normed_v, axis=1, keepdims=True)) / root_mean
    msg_f[:, :Q] = (pack(dslot) / slot_total).astype(bf16)
    for dz in range(1, 4):
        flying.wait(f"loss_z{dz}")
    loss_line = ((loss_z[0] + loss_z[1]) + (loss_z[2] + loss_z[3]))[0:1, 0:1]
    loss_hi = loss_line.astype(bf16).astype(f32)
    loss_mid = (loss_line - loss_hi).astype(bf16).astype(f32)
    lane_f = lax.broadcasted_iota(jnp.int32, (16, LANES), 1)
    extra_f = jnp.where(lane_f == 0, best, 0.0)
    for n, value in enumerate((loss_hi, loss_mid, loss_line - loss_hi - loss_mid)):
        extra_f = jnp.where(lane_f == n + 1, value, extra_f)
    msg_f[:, Q:] = extra_f.astype(bf16)
    to_tok("f", lambda k: msg_f, recv_f, ssem_f, rsem_f)

    flying.wait("f_in")
    flying.wait("keys_z_out")
    for dz in range(4):
        flying.wait(f"keys_cross{dz}_out")
    back = nn(perm[...], recv_f[...].reshape(256, Q + LANES))
    for n in range(PARTS):
        for j in range(4):
            all_keys[0:GROUP, place(n, j)] = back[64 * j : 64 * j + 64, span(n)].astype(bf16)
    factor = jnp.exp(top - back[0:GROUP, Q : Q + 1])
    losses = jnp.sum(back[0:GROUP, Q + 1 : Q + 4], axis=(0, 1), keepdims=True) / OWN
    loss_o[...] = losses / (2.0 * TOK * ROWS * D)

    @pl.loop(0, ROWS // CHUNK)
    def _(n):
        at = pl.multiple_of(n * CHUNK, CHUNK)
        dprob = nt(all_keys[0:GROUP, :], tokens[pl.ds(at, CHUNK), :])
        weights[:, pl.ds(at, CHUNK)] = (terms[:, pl.ds(at, CHUNK)] * factor * dprob).astype(bf16)

    flying.wait("e_in")
    for n in range(PARTS):
        cols = span(n, WIDE)
        part = nn(weights[...], tokens[:, cols])
        for k in range(4):
            part += recv_e[k, :, cols].astype(f32)
        msg_g[n] = spread(lines(part)).reshape(TOK, 16, LANES)
        to_tok(f"g{n}", lambda k: msg_g.at[n, k], recv_g.at[n], ssem_g.at[n], rsem_g.at[n])
    for n in range(PARTS):
        flying.wait(f"g{n}_in")
        unpack(sum_of(recv_g.at[n], TOK) / D**0.5, n)
    grad_o[...] = x16[0:4, :]
    finish()


def hand_over(mixed_in, loss_in, grad_in, mixed_out, loss_out, grad_out, held, sem_in, sem_out):
    blocks = [pl.ds(n * 112, 112) for n in range(4)]
    ins = [pltpu.make_async_copy(mixed_in.at[b], held.at[b], sem_in.at[n]) for n, b in enumerate(blocks)]
    outs = [pltpu.make_async_copy(held.at[b], mixed_out.at[b], sem_out.at[n]) for n, b in enumerate(blocks)]
    for copy in ins:
        copy.start()
    loss_out[...] = loss_in[...]
    grad_out[...] = grad_in[...]
    for n in range(4):
        ins[n].wait()
        outs[n].start()
    for copy in outs:
        copy.wait()


def body(tokens, dispatch_keys, expand_weight, reduce_weight, teacher):
    any_spec = pl.BlockSpec(memory_space=pl.ANY)
    vmem_spec = pl.BlockSpec(memory_space=pltpu.VMEM)
    V = pltpu.VMEM
    dma = pltpu.SemaphoreType.DMA
    out_shape = (
        jax.ShapeDtypeStruct((PART, D), bf16),
        jax.ShapeDtypeStruct((1, 1), f32),
        jax.ShapeDtypeStruct((OWN, D), f32),
    )
    mixed, loss, grad = pl.pallas_call(
        kernel,
        out_shape=out_shape,
        in_specs=[any_spec, vmem_spec, any_spec, any_spec, any_spec],
        out_specs=(any_spec, vmem_spec, vmem_spec),
        scratch_shapes=[
            V((ROWS, D), bf16), V((OWN, D, H), bf16), V((OWN, H, D), bf16), V((PART, D), bf16),
            V((256, 256), bf16), V((256, 256), bf16), V((16, Q), f32),
            V((16, Q), bf16), V((TOK, 16, Q), bf16), V((2 * HALF, D), bf16),
            V((GROUP, ROWS), f32), V((GROUP, ROWS), bf16),
            V((PARTS + 1, TOK, 16, LANES), bf16), V((PARTS + 1, TOK, 16, LANES), bf16),
            V((16, D), f32), V((16, D), f32), V((PARTS, 16, LANES), bf16),
            V((PARTS, 2, 64, 16, LANES), bf16), V((2 * HALF, D), bf16),
            V((PART, 2 * HALF), f32), V((PART, 2 * HALF), bf16), V((PART, D), bf16), V((PART, D), bf16),
            V((HALF, D), f32), V((PARTS, HALF, WIDE), bf16), V((PARTS, HALF, WIDE), bf16),
            V((PARTS, 64, 16, LANES), bf16), V((PARTS, 64, 16, LANES), bf16),
            V((HALF, D), f32), V((PARTS, HALF, WIDE), bf16), V((PARTS, HALF, WIDE), bf16),
            V((4, GROUP, D), bf16), V((4, GROUP, D), bf16),
            V((8, LANES), f32), V((8, LANES), f32), V((4, 8, LANES), f32),
            V((16, Q + LANES), bf16), V((TOK, 16, Q + LANES), bf16),
            V((PARTS, TOK, 16, LANES), bf16), V((PARTS, TOK, 16, LANES), bf16),
            dma((4,)), dma, dma, dma, dma, dma((4,)), dma((4,)), dma((4,)),
            dma((PARTS + 1,)), dma((PARTS + 1,)), dma((PARTS,)), dma((PARTS,)), dma((PARTS,)), dma((PARTS,)),
            dma((PARTS,)), dma((PARTS,)), dma((PARTS,)), dma((PARTS,)), dma((PARTS,)), dma((PARTS,)), dma, dma,
            dma, dma, dma, dma((4,)), dma, dma, dma((PARTS,)), dma((PARTS,)),
        ],
        compiler_params=pltpu.CompilerParams(
            collective_id=0, has_side_effects=True, vmem_limit_bytes=60 * 2**20
        ),
    )(tokens, dispatch_keys, expand_weight, reduce_weight, teacher)
    mixed, loss, grad = pl.pallas_call(
        hand_over,
        out_shape=out_shape,
        in_specs=[any_spec, vmem_spec, vmem_spec],
        out_specs=(any_spec, vmem_spec, vmem_spec),
        scratch_shapes=[V((PART, D), bf16), dma((4,)), dma((4,))],
    )(mixed, loss, grad)
    return mixed, loss.reshape(()), grad


def solution(mesh):
    in_specs = (
        P("tok", None),
        P(("tok", "exp"), None),
        P(("tok", "exp"), None, None),
        P(("tok", "exp"), None, None),
        P(("tok", "exp"), None),
    )
    out_specs = (P(("tok", "exp"), None), P(), P(("tok", "exp"), None))
    return jax.shard_map(body, mesh=mesh, in_specs=in_specs, out_specs=out_specs, check_vma=False)
```

```python
import functools
import jax
import jax.numpy as jnp
from jax import lax
from jax.experimental import pallas as pl
from jax.experimental.pallas import tpu as pltpu
from jax.sharding import PartitionSpec as P

MESH = pl.DeviceIdType.MESH
f32, bf16 = jnp.float32, jnp.bfloat16
D, H, ROWS, PART, OWN, GROUP, HALF = 1536, 512, 3584, 448, 4, 64, 256
TOK = 16
PARTS = 3
WIDE = 512
LANES = 128
Q = PARTS * LANES
CHUNK = 1792
gelu_coef = 0.7978845608028654
cube_coef = 0.044715


def gelu_pair(values):
    tanh_value = jnp.tanh(gelu_coef * (values + cube_coef * values * values * values))
    output = 0.5 * values * (1.0 + tanh_value)
    derivative = 0.5 * (1.0 + tanh_value) + 0.5 * values * (
        1.0 - tanh_value * tanh_value
    ) * gelu_coef * (1.0 + 3.0 * cube_coef * values * values)
    return (output, derivative)


def nn(a, b):
    return lax.dot_general(a, b, (((1,), (0,)), ((), ())), preferred_element_type=f32)


def nt(a, b):
    return lax.dot_general(a, b, (((1,), (1,)), ((), ())), preferred_element_type=f32)


def tn(a, b):
    return lax.dot_general(a, b, (((0,), (0,)), ((), ())), preferred_element_type=f32)


def wait_bytes(ref, sem):
    pltpu.make_async_copy(ref, ref, sem).wait()


class Pending:
    def __init__(self):
        self.open = {}

    def add(self, name, ref, sem):
        self.open[name] = (ref, sem)

    def wait(self, name):
        wait_bytes(*self.open.pop(name))

    def finish(self):
        for name in list(self.open):
            self.wait(name)


def kernel(
    tokens_h, keys, expand_h, reduce_h, teacher_h,
    mixed_h, loss_o, grad_o,
    tokens, expand, reduce_, teacher, perm, perm_t, wide,
    key_msg, recv_k, all_keys,
    terms, weights, msg_b, recv_b,
    normed, x16, out_msg, gath_o, every_out,
    comb, comb_b, grad_rows, mixed,
    half_d, cross_d, arrived_d, msg_d, recv_d,
    half_e, cross_e, arrived_e, fold_e, recv_e, loss_own, loss_other, loss_z,
    msg_f, recv_f, msg_g, recv_g,
    load_sem, mixed_sem, ssem_k, rsem_k, ssem_kz, rsem_kz, csend_k, crecv_k,
    ssem_b, rsem_b, ssem_o, rsem_o, csend_o, crecv_o,
    csend_d, crecv_d, ssem_d, rsem_d, csend_e, crecv_e, ssem_e, rsem_e,
    csend_l, crecv_l, ssem_l, rsem_l, ssem_f, rsem_f, ssem_g, rsem_g,
):
    t = lax.axis_index("tok")
    e = lax.axis_index("exp")
    x, y = t >> 2, t & 3
    z, c = e >> 1, e & 1
    other = (t, z * 2 + 1 - c)
    flying = Pending()
    finish = flying.finish

    def offset(d):
        return 2 - 2 * (d & 1) + ((d + (d >> 1)) & 1)

    def peer(k):
        t2 = ((x + offset((k >> 2) & 3)) & 3) * 4 + ((y + offset(k & 3)) & 3)
        return t2, (z + offset(k >> 4)) & 3

    def peer_tok(k):
        return peer(k + 48)[0]

    barrier = pltpu.get_barrier_semaphore()

    def greet(k, carry):
        t2, z2 = peer(k)
        pl.semaphore_signal(barrier, inc=1, device_id=(t2, z2 * 2 + c), device_id_type=MESH)
        return carry

    lax.fori_loop(0, 63, greet, 0)
    pl.semaphore_signal(barrier, inc=1, device_id=other, device_id_type=MESH)

    for n, (name, src, dst) in enumerate((
        ("tokens", tokens_h, tokens), ("expand", expand_h, expand),
        ("reduce", reduce_h, reduce_), ("teacher", teacher_h, teacher),
    )):
        pltpu.make_async_copy(src, dst, load_sem.at[n]).start()
        flying.add(name, dst, load_sem.at[n])

    row = lax.broadcasted_iota(jnp.int32, (256, 256), 0)
    col = lax.broadcasted_iota(jnp.int32, (256, 256), 1)

    def moved(r):
        return ((r >> 2) & 15) * 16 + (r >> 6) * 4 + (r & 3)

    perm[...] = jnp.where(col == moved(row), 1.0, 0.0).astype(bf16)
    perm_t[...] = jnp.where(row == moved(col), 1.0, 0.0).astype(bf16)

    def place(n, j):
        return slice(WIDE * n + LANES * j, WIDE * n + LANES * j + LANES)

    def span(n, width=LANES):
        return slice(width * n, width * n + width)

    def pack(value):
        for n in range(PARTS):
            for j in range(4):
                wide[4 * j : 4 * j + 4, span(n)] = value[0:4, place(n, j)]
        return wide[...]

    def unpack(message, n):
        wide[:, span(n)] = message
        for j in range(4):
            x16[0:4, place(n, j)] = wide[4 * j : 4 * j + 4, span(n)]

    def lines(value):
        return jnp.concatenate([value[:, span(j)] for j in range(4)], axis=0).astype(bf16)

    def spread(stacked):
        return nn(perm_t[...], stacked).astype(bf16)

    def remote(src, dst, send, recv, device):
        pltpu.make_async_remote_copy(
            src, dst, send, recv, device_id=device, device_id_type=MESH
        ).start()

    def cross(name, src, dst, send, recv):
        remote(src, dst, send, recv, other)
        flying.add(name + "_out", src, send)
        flying.add(name + "_in", dst, recv)

    def to_tok(name, src_of, recv_ref, send, recv):
        pltpu.make_async_copy(src_of(t), recv_ref.at[t], recv).start()

        def step(k, carry):
            t2 = peer_tok(k)
            remote(src_of(t2), recv_ref.at[t], send, recv, (t2, e))
            return carry

        lax.fori_loop(0, TOK - 1, step, 0)
        flying.add(name + "_out", recv_ref.at[pl.ds(0, TOK - 1)], send)
        flying.add(name + "_in", recv_ref, recv)

    def to_all(name, src_of, recv_ref, send, recv):
        me = z * TOK + t
        pltpu.make_async_copy(src_of(me), recv_ref.at[me], recv).start()

        def step(k, carry):
            t2, z2 = peer(k)
            remote(src_of(z2 * TOK + t2), recv_ref.at[me], send, recv, (t2, z2 * 2 + c))
            return carry

        lax.fori_loop(0, 63, step, 0)
        flying.add(name + "_out", recv_ref.at[pl.ds(0, 63)], send)
        flying.add(name + "_in", recv_ref, recv)

    def to_z(name, src_of, dst, send, recv, three):
        for dz in range(1, 4):
            z2 = (z + dz) & 3
            remote(src_of(z2), dst, send, recv, (t, z2 * 2 + c))
        flying.add(name + "_out", three, send)

    def sum_of(ref, count):
        return lax.fori_loop(
            0, count, lambda k, s: s + ref[k].astype(f32), jnp.zeros(ref.shape[1:], f32)
        )

    x16[...] = jnp.zeros((16, D), f32)
    key_msg[...] = pack(keys[...].astype(f32)).astype(bf16)
    pl.semaphore_wait(barrier, 64)

    to_tok("keys", lambda k: key_msg, recv_k, ssem_k, rsem_k)
    flying.wait("keys_in")
    mine = pl.ds(pl.multiple_of(z * GROUP, GROUP), GROUP)
    moved_k = nn(perm[...], recv_k[...].reshape(256, Q)).astype(bf16)
    for n in range(PARTS):
        for j in range(4):
            all_keys[mine, place(n, j)] = moved_k[64 * j : 64 * j + 64, span(n)]

    def key_rows(half, dz):
        return pl.ds(pl.multiple_of(half * HALF + ((z + dz) & 3) * GROUP, GROUP), GROUP)

    def key_cross(dz):
        zz = (z + dz) & 3
        cross(
            f"keys_cross{dz}", all_keys.at[key_rows(0, dz)], all_keys.at[key_rows(1, dz)],
            csend_k.at[zz], crecv_k.at[zz],
        )

    to_z(
        "keys_z", lambda z2: all_keys.at[mine], all_keys.at[mine], ssem_kz, rsem_kz.at[z],
        all_keys.at[pl.ds(0, 3 * GROUP)],
    )
    for dz in range(1, 4):
        flying.add(f"keys_z{dz}", all_keys.at[key_rows(0, dz)], rsem_kz.at[(z + dz) & 3])
    key_cross(0)
    flying.wait("tokens")

    @pl.loop(0, ROWS // CHUNK)
    def _(n):
        at = pl.multiple_of(n * CHUNK, CHUNK)
        terms[:, pl.ds(at, CHUNK)] = nt(all_keys[mine, :], tokens[pl.ds(at, CHUNK), :])

    top = jnp.max(terms[...], axis=1, keepdims=True).astype(bf16).astype(f32)
    exp_terms = jnp.exp(terms[...] - top)
    terms[...] = exp_terms
    weights[...] = exp_terms.astype(bf16)
    total = jnp.sum(exp_terms, axis=1, keepdims=True)
    lane = lax.broadcasted_iota(jnp.int32, (GROUP, LANES), 1)
    total_hi = total.astype(bf16).astype(f32)
    extra = jnp.where(
        lane == 0, top, jnp.where(lane == 1, total_hi, jnp.where(lane == 2, total - total_hi, 0.0))
    )
    extra_b = extra.astype(bf16)
    msg_b[PARTS] = spread(jnp.concatenate([extra_b] * 4, axis=0)).reshape(TOK, 16, LANES)
    to_tok("b3", lambda k: msg_b.at[PARTS, k], recv_b.at[PARTS], ssem_b.at[PARTS], rsem_b.at[PARTS])
    for n in range(PARTS):
        part = nn(weights[...], tokens[:, span(n, WIDE)])
        msg_b[n] = spread(lines(part)).reshape(TOK, 16, LANES)
        to_tok(f"b{n}", lambda k: msg_b.at[n, k], recv_b.at[n], ssem_b.at[n], rsem_b.at[n])

    for dz in range(1, 4):
        flying.wait(f"keys_z{dz}")
        key_cross(dz)
    for dz in range(4):
        flying.wait(f"keys_cross{dz}_in")
    local = tokens.at[pl.ds(pl.multiple_of(e * PART, GROUP), PART)]
    scores = nt(local[...], all_keys[...])
    row_terms = jnp.exp(scores - jnp.max(scores, axis=1, keepdims=True))
    comb_v = row_terms / jnp.sum(row_terms, axis=1, keepdims=True)
    comb[...] = comb_v
    comb_b[...] = comb_v.astype(bf16)

    flying.wait("b3_in")
    best = recv_b[PARTS, 0, :, 0:1].astype(f32)
    for k in range(1, TOK):
        best = jnp.maximum(best, recv_b[PARTS, k, :, 0:1].astype(f32))
    scales = []
    slot_total = jnp.zeros((16, 1), f32)
    for k in range(TOK):
        held = recv_b[PARTS, k].astype(f32)
        scales.append(jnp.exp(held[:, 0:1] - best))
        slot_total += scales[k] * (held[:, 1:2] + held[:, 2:3])
    for n in range(PARTS):
        flying.wait(f"b{n}_in")
        slot_sum = jnp.zeros((16, LANES), f32)
        for k in range(TOK):
            slot_sum += scales[k] * recv_b[n, k].astype(f32)
        unpack(slot_sum / slot_total, n)
    slot_in = x16[...]
    root_mean = jnp.sqrt(jnp.mean(slot_in * slot_in, axis=1, keepdims=True) + 1e-06)
    normed_v = slot_in / root_mean
    normed[...] = normed_v
    normed_b = normed_v.astype(bf16)

    flying.wait("expand")
    flying.wait("reduce")
    row_h = lax.broadcasted_iota(jnp.int32, (16, H), 0)
    row_d = lax.broadcasted_iota(jnp.int32, (16, D), 0)
    pre_act = jnp.zeros((16, H), f32)
    for s in range(OWN):
        pre_act = jnp.where(row_h == s, nn(normed_b, expand[s]), pre_act)
    act_value, gelu_slope = gelu_pair(pre_act)
    act_b = act_value.astype(bf16)
    slot_out = jnp.zeros((16, D), f32)
    for s in range(OWN):
        slot_out = jnp.where(row_d == s, nn(act_b, reduce_[s]), slot_out)
    packed_out = pack(slot_out).astype(bf16)
    for n in range(PARTS):
        out_msg[n] = packed_out[:, span(n)]
    for n in range(PARTS):
        to_all(f"o{n}", lambda k: out_msg.at[n], gath_o.at[n, 0], ssem_o.at[n], rsem_o.at[n])

    flying.wait("teacher")

    def settle(n, half):
        block = jnp.concatenate(
            [gath_o[n, half, span(g, TOK)].reshape(256, LANES) for g in range(4)], axis=1
        )
        r = nn(perm[...], block).astype(bf16)
        for g in range(4):
            for j in range(4):
                every_out[half * HALF + g * GROUP : half * HALF + (g + 1) * GROUP, place(n, j)] = r[
                    64 * j : 64 * j + 64, span(g)
                ]

    def pass_on(n):
        flying.wait(f"o{n}_in")
        cross(f"o_cross{n}", gath_o.at[n, 0], gath_o.at[n, 1], csend_o.at[n], crecv_o.at[n])
        settle(n, 0)

    def combine(n):
        flying.wait(f"o_cross{n}_in")
        settle(n, 1)
        cols = span(n, WIDE)
        result = nn(comb_b[...], every_out[:, cols])
        mixed[:, cols] = result.astype(bf16)
        misfit = result - teacher[:, cols].astype(f32)
        grad_v = (misfit / D).astype(bf16)
        grad_rows[:, cols] = grad_v
        out_part = tn(comb_b[...], grad_v)
        half_d[:, cols] = out_part[:HALF]
        cross_d[n] = out_part[HALF:].astype(bf16)
        cross(f"d_cross{n}", cross_d.at[n], arrived_d.at[n], csend_d.at[n], crecv_d.at[n])
        return jnp.sum(misfit * misfit)

    def send_d(n):
        flying.wait(f"d_cross{n}_in")
        whole = half_d[:, span(n, WIDE)] + arrived_d[n].astype(f32)
        stacked = jnp.concatenate([lines(whole[span(g, GROUP)]) for g in range(4)], axis=1)
        r = spread(stacked)
        for g in range(4):
            msg_d[n, span(g, TOK)] = r[:, span(g)].reshape(TOK, 16, LANES)
        to_all(f"d{n}", lambda k: msg_d.at[n, k], recv_d.at[n], ssem_d.at[n], rsem_d.at[n])

    pass_on(0)
    loss_sum = combine(0)
    pass_on(1)
    send_d(0)
    loss_sum += combine(1)
    pass_on(2)
    send_d(1)
    loss_sum += combine(2)
    loss_own[...] = jnp.full((8, LANES), loss_sum, f32)
    cross("loss", loss_own, loss_other, csend_l, crecv_l)
    send_d(2)
    pltpu.make_async_copy(mixed, mixed_h, mixed_sem).start()
    flying.add("mixed", mixed, mixed_sem)

    dcomb = nt(grad_rows[...], every_out[...])
    weighted_d = comb[...] * dcomb
    dscore = (weighted_d - comb[...] * jnp.sum(weighted_d, axis=1, keepdims=True)).astype(bf16)
    for n in range(PARTS):
        key_part = tn(dscore, local[:, span(n, WIDE)])
        half_e[:, span(n, WIDE)] = key_part[:HALF]
        cross_e[n] = key_part[HALF:].astype(bf16)
        cross(f"e_cross{n}", cross_e.at[n], arrived_e.at[n], csend_e.at[n], crecv_e.at[n])
    flying.wait("loss_in")
    loss_z[z] = loss_own[...] + loss_other[...]
    to_z("loss_z", lambda z2: loss_z.at[z], loss_z.at[z], ssem_l, rsem_l.at[z], loss_z.at[pl.ds(0, 3)])
    for dz in range(1, 4):
        flying.add(f"loss_z{dz}", loss_z.at[(z + dz) & 3], rsem_l.at[(z + dz) & 3])
    for n in range(PARTS):
        flying.wait(f"e_cross{n}_in")
        whole_e = (half_e[:, span(n, WIDE)] + arrived_e[n].astype(f32)).astype(bf16)
        for g in range(4):
            fold_e[g, :, span(n, WIDE)] = whole_e[span(g, GROUP)]
    to_z("e", lambda z2: fold_e.at[z2], recv_e.at[z], ssem_e, rsem_e, fold_e.at[pl.ds(0, 3)])
    pltpu.make_async_copy(fold_e.at[z], recv_e.at[z], rsem_e).start()
    flying.add("e_in", recv_e, rsem_e)

    dact = jnp.zeros((16, H), f32)
    for n in range(PARTS):
        flying.wait(f"d{n}_in")
        unpack(sum_of(recv_d.at[n], 64), n)
        cols = span(n, WIDE)
        out_grad = x16[:, cols].astype(bf16)
        for s in range(OWN):
            dact = jnp.where(row_h == s, dact + nt(out_grad, reduce_[s, :, cols]), dact)
    dpre = (dact * gelu_slope).astype(bf16)
    dnormed = jnp.zeros((16, D), f32)
    for s in range(OWN):
        dnormed = jnp.where(row_d == s, nt(dpre, expand[s]), dnormed)
    normed_v = normed[...]
    dslot = (dnormed - normed_v * jnp.mean(dnormed * normed_v, axis=1, keepdims=True)) / root_mean
    msg_f[:, :Q] = (pack(dslot) / slot_total).astype(bf16)
    for dz in range(1, 4):
        flying.wait(f"loss_z{dz}")
    loss_line = ((loss_z[0] + loss_z[1]) + (loss_z[2] + loss_z[3]))[0:1, 0:1]
    loss_hi = loss_line.astype(bf16).astype(f32)
    loss_mid = (loss_line - loss_hi).astype(bf16).astype(f32)
    lane_f = lax.broadcasted_iota(jnp.int32, (16, LANES), 1)
    extra_f = jnp.where(lane_f == 0, best, 0.0)
    for n, value in enumerate((loss_hi, loss_mid, loss_line - loss_hi - loss_mid)):
        extra_f = jnp.where(lane_f == n + 1, value, extra_f)
    msg_f[:, Q:] = extra_f.astype(bf16)
    to_tok("f", lambda k: msg_f, recv_f, ssem_f, rsem_f)

    flying.wait("f_in")
    flying.wait("keys_z_out")
    for dz in range(4):
        flying.wait(f"keys_cross{dz}_out")
    back = nn(perm[...], recv_f[...].reshape(256, Q + LANES))
    for n in range(PARTS):
        for j in range(4):
            all_keys[0:GROUP, place(n, j)] = back[64 * j : 64 * j + 64, span(n)].astype(bf16)
    factor = jnp.exp(top - back[0:GROUP, Q : Q + 1])
    losses = jnp.sum(back[0:GROUP, Q + 1 : Q + 4], axis=(0, 1), keepdims=True) / OWN
    loss_o[...] = losses / (2.0 * TOK * ROWS * D)

    @pl.loop(0, ROWS // CHUNK)
    def _(n):
        at = pl.multiple_of(n * CHUNK, CHUNK)
        dprob = nt(all_keys[0:GROUP, :], tokens[pl.ds(at, CHUNK), :])
        weights[:, pl.ds(at, CHUNK)] = (terms[:, pl.ds(at, CHUNK)] * factor * dprob).astype(bf16)

    flying.wait("e_in")
    for n in range(PARTS):
        cols = span(n, WIDE)
        part = nn(weights[...], tokens[:, cols])
        for k in range(4):
            part += recv_e[k, :, cols].astype(f32)
        msg_g[n] = spread(lines(part)).reshape(TOK, 16, LANES)
        to_tok(f"g{n}", lambda k: msg_g.at[n, k], recv_g.at[n], ssem_g.at[n], rsem_g.at[n])
    for n in range(PARTS):
        flying.wait(f"g{n}_in")
        unpack(sum_of(recv_g.at[n], TOK) / D**0.5, n)
    grad_o[...] = x16[0:4, :]
    finish()


def hand_over(*refs):
    ins, outs, held, (sem_in, sem_out) = refs[:3], refs[3:6], refs[6:9], refs[9:]
    rows = [pl.ds(n * 112, 112) for n in range(4)]
    steps = [(ins[k], held[k], outs[k]) for k in (1, 2)]
    steps += [tuple(r.at[b] for r in (ins[0], held[0], outs[0])) for b in rows]
    first = [pltpu.make_async_copy(a, b, sem_in.at[n]) for n, (a, b, _) in enumerate(steps)]
    second = [pltpu.make_async_copy(b, c, sem_out.at[n]) for n, (_, b, c) in enumerate(steps)]
    for copy in first:
        copy.start()
    for n in range(len(steps)):
        first[n].wait()
        second[n].start()
    for copy in second:
        copy.wait()


def body(tokens, dispatch_keys, expand_weight, reduce_weight, teacher):
    any_spec = pl.BlockSpec(memory_space=pl.ANY)
    vmem_spec = pl.BlockSpec(memory_space=pltpu.VMEM)
    V = pltpu.VMEM
    dma = pltpu.SemaphoreType.DMA
    out_shape = (
        jax.ShapeDtypeStruct((PART, D), bf16),
        jax.ShapeDtypeStruct((1, 1), f32),
        jax.ShapeDtypeStruct((OWN, D), f32),
    )
    mixed, loss, grad = pl.pallas_call(
        kernel,
        out_shape=out_shape,
        in_specs=[any_spec, vmem_spec, any_spec, any_spec, any_spec],
        out_specs=(any_spec, vmem_spec, vmem_spec),
        scratch_shapes=[
            V((ROWS, D), bf16), V((OWN, D, H), bf16), V((OWN, H, D), bf16), V((PART, D), bf16),
            V((256, 256), bf16), V((256, 256), bf16), V((16, Q), f32),
            V((16, Q), bf16), V((TOK, 16, Q), bf16), V((2 * HALF, D), bf16),
            V((GROUP, ROWS), f32), V((GROUP, ROWS), bf16),
            V((PARTS + 1, TOK, 16, LANES), bf16), V((PARTS + 1, TOK, 16, LANES), bf16),
            V((16, D), f32), V((16, D), f32), V((PARTS, 16, LANES), bf16),
            V((PARTS, 2, 64, 16, LANES), bf16), V((2 * HALF, D), bf16),
            V((PART, 2 * HALF), f32), V((PART, 2 * HALF), bf16), V((PART, D), bf16), V((PART, D), bf16),
            V((HALF, D), f32), V((PARTS, HALF, WIDE), bf16), V((PARTS, HALF, WIDE), bf16),
            V((PARTS, 64, 16, LANES), bf16), V((PARTS, 64, 16, LANES), bf16),
            V((HALF, D), f32), V((PARTS, HALF, WIDE), bf16), V((PARTS, HALF, WIDE), bf16),
            V((4, GROUP, D), bf16), V((4, GROUP, D), bf16),
            V((8, LANES), f32), V((8, LANES), f32), V((4, 8, LANES), f32),
            V((16, Q + LANES), bf16), V((TOK, 16, Q + LANES), bf16),
            V((PARTS, TOK, 16, LANES), bf16), V((PARTS, TOK, 16, LANES), bf16),
            dma((4,)), dma, dma, dma, dma, dma((4,)), dma((4,)), dma((4,)),
            dma((PARTS + 1,)), dma((PARTS + 1,)), dma((PARTS,)), dma((PARTS,)), dma((PARTS,)), dma((PARTS,)),
            dma((PARTS,)), dma((PARTS,)), dma((PARTS,)), dma((PARTS,)), dma((PARTS,)), dma((PARTS,)), dma, dma,
            dma, dma, dma, dma((4,)), dma, dma, dma((PARTS,)), dma((PARTS,)),
        ],
        compiler_params=pltpu.CompilerParams(
            collective_id=0, has_side_effects=True, vmem_limit_bytes=56 * 2**20
        ),
    )(tokens, dispatch_keys, expand_weight, reduce_weight, teacher)
    mixed, loss, grad = pl.pallas_call(
        hand_over,
        out_shape=out_shape,
        in_specs=[any_spec] * 3,
        out_specs=(any_spec,) * 3,
        scratch_shapes=[V(o.shape, o.dtype) for o in out_shape] + [dma((6,)), dma((6,))],
    )(mixed, loss, grad)
    return mixed, loss.reshape(()), grad


def solution(mesh):
    in_specs = (
        P("tok", None),
        P(("tok", "exp"), None),
        P(("tok", "exp"), None, None),
        P(("tok", "exp"), None, None),
        P(("tok", "exp"), None),
    )
    out_specs = (P(("tok", "exp"), None), P(), P(("tok", "exp"), None))
    return jax.shard_map(body, mesh=mesh, in_specs=in_specs, out_specs=out_specs, check_vma=False)
```

```python
import functools
import jax
import jax.numpy as jnp
from jax import lax
from jax.experimental import pallas as pl
from jax.experimental.pallas import tpu as pltpu
from jax.sharding import PartitionSpec as P

MESH = pl.DeviceIdType.MESH
f32, bf16 = jnp.float32, jnp.bfloat16
D, H, ROWS, PART, OWN, GROUP, HALF = 1536, 512, 3584, 448, 4, 64, 256
TOK = 16
PARTS = 3
WIDE = 512
LANES = 128
Q = PARTS * LANES
CHUNK = 3584
gelu_coef = 0.7978845608028654
cube_coef = 0.044715


def gelu_pair(values):
    tanh_value = jnp.tanh(gelu_coef * (values + cube_coef * values * values * values))
    output = 0.5 * values * (1.0 + tanh_value)
    derivative = 0.5 * (1.0 + tanh_value) + 0.5 * values * (
        1.0 - tanh_value * tanh_value
    ) * gelu_coef * (1.0 + 3.0 * cube_coef * values * values)
    return (output, derivative)


def nn(a, b):
    return lax.dot_general(a, b, (((1,), (0,)), ((), ())), preferred_element_type=f32)


def nt(a, b):
    return lax.dot_general(a, b, (((1,), (1,)), ((), ())), preferred_element_type=f32)


def tn(a, b):
    return lax.dot_general(a, b, (((0,), (0,)), ((), ())), preferred_element_type=f32)


def wait_bytes(ref, sem):
    pltpu.make_async_copy(ref, ref, sem).wait()


class Pending:
    def __init__(self):
        self.open = {}

    def add(self, name, ref, sem):
        self.open[name] = (ref, sem)

    def wait(self, name):
        wait_bytes(*self.open.pop(name))

    def finish(self):
        for name in list(self.open):
            self.wait(name)


def kernel(
    tokens_h, keys, expand_h, reduce_h, teacher_h,
    mixed_h, loss_o, grad_o,
    tokens, expand, reduce_, teacher, perm, perm_t, wide,
    key_msg, recv_k, all_keys,
    terms, weights, msg_b, recv_b,
    normed, x16, out_msg, gath_o, every_out,
    comb, comb_b, grad_rows, mixed,
    half_d, cross_d, arrived_d, msg_d, recv_d,
    half_e, cross_e, arrived_e, fold_e, recv_e, loss_own, loss_other, loss_z,
    msg_f, recv_f, msg_g, recv_g,
    load_sem, mixed_sem, ssem_k, rsem_k, ssem_kz, rsem_kz, csend_k, crecv_k,
    ssem_b, rsem_b, ssem_o, rsem_o, csend_o, crecv_o,
    csend_d, crecv_d, ssem_d, rsem_d, csend_e, crecv_e, ssem_e, rsem_e,
    csend_l, crecv_l, ssem_l, rsem_l, ssem_f, rsem_f, ssem_g, rsem_g,
):
    t = lax.axis_index("tok")
    e = lax.axis_index("exp")
    x, y = t >> 2, t & 3
    z, c = e >> 1, e & 1
    other = (t, z * 2 + 1 - c)
    flying = Pending()
    finish = flying.finish

    def offset(d):
        return 2 - 2 * (d & 1) + ((d + (d >> 1)) & 1)

    def peer(k):
        t2 = ((x + offset((k >> 2) & 3)) & 3) * 4 + ((y + offset(k & 3)) & 3)
        return t2, (z + offset(k >> 4)) & 3

    def peer_tok(k):
        return peer(k + 48)[0]

    barrier = pltpu.get_barrier_semaphore()

    def greet(k, carry):
        t2, z2 = peer(k)
        pl.semaphore_signal(barrier, inc=1, device_id=(t2, z2 * 2 + c), device_id_type=MESH)
        return carry

    lax.fori_loop(0, 63, greet, 0, unroll=9)
    pl.semaphore_signal(barrier, inc=1, device_id=other, device_id_type=MESH)

    for n, (name, src, dst) in enumerate((
        ("tokens", tokens_h, tokens), ("expand", expand_h, expand),
        ("reduce", reduce_h, reduce_), ("teacher", teacher_h, teacher),
    )):
        pltpu.make_async_copy(src, dst, load_sem.at[n]).start()
        flying.add(name, dst, load_sem.at[n])

    row = lax.broadcasted_iota(jnp.int32, (256, 256), 0)
    col = lax.broadcasted_iota(jnp.int32, (256, 256), 1)

    def moved(r):
        return ((r >> 2) & 15) * 16 + (r >> 6) * 4 + (r & 3)

    perm[...] = jnp.where(col == moved(row), 1.0, 0.0).astype(bf16)
    perm_t[...] = jnp.where(row == moved(col), 1.0, 0.0).astype(bf16)

    def place(n, j):
        return slice(WIDE * n + LANES * j, WIDE * n + LANES * j + LANES)

    def span(n, width=LANES):
        return slice(width * n, width * n + width)

    def pack(value):
        for n in range(PARTS):
            for j in range(4):
                wide[4 * j : 4 * j + 4, span(n)] = value[0:4, place(n, j)]
        return wide[...]

    def unpack(message, n):
        wide[:, span(n)] = message
        for j in range(4):
            x16[0:4, place(n, j)] = wide[4 * j : 4 * j + 4, span(n)]

    def lines(value):
        return jnp.concatenate([value[:, span(j)] for j in range(4)], axis=0).astype(bf16)

    def spread(stacked):
        return nn(perm_t[...], stacked).astype(bf16)

    def remote(src, dst, send, recv, device):
        pltpu.make_async_remote_copy(
            src, dst, send, recv, device_id=device, device_id_type=MESH
        ).start()

    def cross(name, src, dst, send, recv):
        remote(src, dst, send, recv, other)
        flying.add(name + "_out", src, send)
        flying.add(name + "_in", dst, recv)

    def to_tok(name, src_of, recv_ref, send, recv):
        pltpu.make_async_copy(src_of(t), recv_ref.at[t], recv).start()

        def step(k, carry):
            t2 = peer_tok(k)
            remote(src_of(t2), recv_ref.at[t], send, recv, (t2, e))
            return carry

        lax.fori_loop(0, TOK - 1, step, 0, unroll=True)
        flying.add(name + "_out", recv_ref.at[pl.ds(0, TOK - 1)], send)
        flying.add(name + "_in", recv_ref, recv)

    def to_all(name, src_of, recv_ref, send, recv):
        me = z * TOK + t
        pltpu.make_async_copy(src_of(me), recv_ref.at[me], recv).start()

        def step(k, carry):
            t2, z2 = peer(k)
            remote(src_of(z2 * TOK + t2), recv_ref.at[me], send, recv, (t2, z2 * 2 + c))
            return carry

        lax.fori_loop(0, 63, step, 0, unroll=9)
        flying.add(name + "_out", recv_ref.at[pl.ds(0, 63)], send)
        flying.add(name + "_in", recv_ref, recv)

    def to_z(name, src_of, dst, send, recv, three):
        for dz in range(1, 4):
            z2 = (z + dz) & 3
            remote(src_of(z2), dst, send, recv, (t, z2 * 2 + c))
        flying.add(name + "_out", three, send)

    def sum_of(ref, count):
        return lax.fori_loop(
            0, count, lambda k, s: s + ref[k].astype(f32), jnp.zeros(ref.shape[1:], f32), unroll=8
        )

    x16[...] = jnp.zeros((16, D), f32)
    key_msg[...] = pack(keys[...].astype(f32)).astype(bf16)
    pl.semaphore_wait(barrier, 64)

    to_tok("keys", lambda k: key_msg, recv_k, ssem_k, rsem_k)
    flying.wait("keys_in")
    mine = pl.ds(pl.multiple_of(z * GROUP, GROUP), GROUP)
    moved_k = nn(perm[...], recv_k[...].reshape(256, Q)).astype(bf16)
    for n in range(PARTS):
        for j in range(4):
            all_keys[mine, place(n, j)] = moved_k[64 * j : 64 * j + 64, span(n)]

    def key_rows(half, dz):
        return pl.ds(pl.multiple_of(half * HALF + ((z + dz) & 3) * GROUP, GROUP), GROUP)

    def key_cross(dz):
        zz = (z + dz) & 3
        cross(
            f"keys_cross{dz}", all_keys.at[key_rows(0, dz)], all_keys.at[key_rows(1, dz)],
            csend_k.at[zz], crecv_k.at[zz],
        )

    to_z(
        "keys_z", lambda z2: all_keys.at[mine], all_keys.at[mine], ssem_kz, rsem_kz.at[z],
        all_keys.at[pl.ds(0, 3 * GROUP)],
    )
    for dz in range(1, 4):
        flying.add(f"keys_z{dz}", all_keys.at[key_rows(0, dz)], rsem_kz.at[(z + dz) & 3])
    key_cross(0)
    flying.wait("tokens")

    @pl.loop(0, ROWS // CHUNK)
    def _(n):
        at = pl.multiple_of(n * CHUNK, CHUNK)
        terms[:, pl.ds(at, CHUNK)] = nt(all_keys[mine, :], tokens[pl.ds(at, CHUNK), :])

    top = jnp.max(terms[...], axis=1, keepdims=True).astype(bf16).astype(f32)
    exp_terms = jnp.exp(terms[...] - top)
    terms[...] = exp_terms
    weights[...] = exp_terms.astype(bf16)
    total = jnp.sum(exp_terms, axis=1, keepdims=True)
    lane = lax.broadcasted_iota(jnp.int32, (GROUP, LANES), 1)
    total_hi = total.astype(bf16).astype(f32)
    extra = jnp.where(
        lane == 0, top, jnp.where(lane == 1, total_hi, jnp.where(lane == 2, total - total_hi, 0.0))
    )
    extra_b = extra.astype(bf16)
    msg_b[PARTS] = spread(jnp.concatenate([extra_b] * 4, axis=0)).reshape(TOK, 16, LANES)
    to_tok("b3", lambda k: msg_b.at[PARTS, k], recv_b.at[PARTS], ssem_b.at[PARTS], rsem_b.at[PARTS])
    for n in range(PARTS):
        part = nn(weights[...], tokens[:, span(n, WIDE)])
        msg_b[n] = spread(lines(part)).reshape(TOK, 16, LANES)
        to_tok(f"b{n}", lambda k: msg_b.at[n, k], recv_b.at[n], ssem_b.at[n], rsem_b.at[n])

    for dz in range(1, 4):
        flying.wait(f"keys_z{dz}")
        key_cross(dz)
    for dz in range(4):
        flying.wait(f"keys_cross{dz}_in")
    local = tokens.at[pl.ds(pl.multiple_of(e * PART, GROUP), PART)]
    scores = nt(local[...], all_keys[...])
    row_terms = jnp.exp(scores - jnp.max(scores, axis=1, keepdims=True))
    comb_v = row_terms / jnp.sum(row_terms, axis=1, keepdims=True)
    comb[...] = comb_v
    comb_b[...] = comb_v.astype(bf16)

    flying.wait("b3_in")
    best = recv_b[PARTS, 0, :, 0:1].astype(f32)
    for k in range(1, TOK):
        best = jnp.maximum(best, recv_b[PARTS, k, :, 0:1].astype(f32))
    scales = []
    slot_total = jnp.zeros((16, 1), f32)
    for k in range(TOK):
        held = recv_b[PARTS, k].astype(f32)
        scales.append(jnp.exp(held[:, 0:1] - best))
        slot_total += scales[k] * (held[:, 1:2] + held[:, 2:3])
    for n in range(PARTS):
        flying.wait(f"b{n}_in")
        slot_sum = jnp.zeros((16, LANES), f32)
        for k in range(TOK):
            slot_sum += scales[k] * recv_b[n, k].astype(f32)
        unpack(slot_sum / slot_total, n)
    slot_in = x16[...]
    root_mean = jnp.sqrt(jnp.mean(slot_in * slot_in, axis=1, keepdims=True) + 1e-06)
    normed_v = slot_in / root_mean
    normed[...] = normed_v
    normed_b = normed_v.astype(bf16)

    flying.wait("expand")
    flying.wait("reduce")
    row_h = lax.broadcasted_iota(jnp.int32, (16, H), 0)
    row_d = lax.broadcasted_iota(jnp.int32, (16, D), 0)
    pre_act = jnp.zeros((16, H), f32)
    for s in range(OWN):
        pre_act = jnp.where(row_h == s, nn(normed_b, expand[s]), pre_act)
    act_value, gelu_slope = gelu_pair(pre_act)
    act_b = act_value.astype(bf16)
    slot_out = jnp.zeros((16, D), f32)
    for s in range(OWN):
        slot_out = jnp.where(row_d == s, nn(act_b, reduce_[s]), slot_out)
    packed_out = pack(slot_out).astype(bf16)
    for n in range(PARTS):
        out_msg[n] = packed_out[:, span(n)]
    for n in range(PARTS):
        to_all(f"o{n}", lambda k: out_msg.at[n], gath_o.at[n, 0], ssem_o.at[n], rsem_o.at[n])

    flying.wait("teacher")

    def settle(n, half):
        block = jnp.concatenate(
            [gath_o[n, half, span(g, TOK)].reshape(256, LANES) for g in range(4)], axis=1
        )
        r = nn(perm[...], block).astype(bf16)
        for g in range(4):
            for j in range(4):
                every_out[half * HALF + g * GROUP : half * HALF + (g + 1) * GROUP, place(n, j)] = r[
                    64 * j : 64 * j + 64, span(g)
                ]

    def pass_on(n):
        flying.wait(f"o{n}_in")
        cross(f"o_cross{n}", gath_o.at[n, 0], gath_o.at[n, 1], csend_o.at[n], crecv_o.at[n])
        settle(n, 0)

    def combine(n):
        flying.wait(f"o_cross{n}_in")
        settle(n, 1)
        cols = span(n, WIDE)
        result = nn(comb_b[...], every_out[:, cols])
        mixed[:, cols] = result.astype(bf16)
        misfit = result - teacher[:, cols].astype(f32)
        grad_v = (misfit / D).astype(bf16)
        grad_rows[:, cols] = grad_v
        out_part = tn(comb_b[...], grad_v)
        half_d[:, cols] = out_part[:HALF]
        cross_d[n] = out_part[HALF:].astype(bf16)
        cross(f"d_cross{n}", cross_d.at[n], arrived_d.at[n], csend_d.at[n], crecv_d.at[n])
        return jnp.sum(misfit * misfit)

    def send_d(n):
        flying.wait(f"d_cross{n}_in")
        whole = half_d[:, span(n, WIDE)] + arrived_d[n].astype(f32)
        stacked = jnp.concatenate([lines(whole[span(g, GROUP)]) for g in range(4)], axis=1)
        r = spread(stacked)
        for g in range(4):
            msg_d[n, span(g, TOK)] = r[:, span(g)].reshape(TOK, 16, LANES)
        to_all(f"d{n}", lambda k: msg_d.at[n, k], recv_d.at[n], ssem_d.at[n], rsem_d.at[n])

    pass_on(0)
    loss_sum = combine(0)
    pass_on(1)
    send_d(0)
    loss_sum += combine(1)
    pass_on(2)
    send_d(1)
    loss_sum += combine(2)
    loss_own[...] = jnp.full((8, LANES), loss_sum, f32)
    cross("loss", loss_own, loss_other, csend_l, crecv_l)
    send_d(2)
    pltpu.make_async_copy(mixed, mixed_h, mixed_sem).start()
    flying.add("mixed", mixed, mixed_sem)

    dcomb = nt(grad_rows[...], every_out[...])
    weighted_d = comb[...] * dcomb
    dscore = (weighted_d - comb[...] * jnp.sum(weighted_d, axis=1, keepdims=True)).astype(bf16)
    for n in range(PARTS):
        key_part = tn(dscore, local[:, span(n, WIDE)])
        half_e[:, span(n, WIDE)] = key_part[:HALF]
        cross_e[n] = key_part[HALF:].astype(bf16)
        cross(f"e_cross{n}", cross_e.at[n], arrived_e.at[n], csend_e.at[n], crecv_e.at[n])
    flying.wait("loss_in")
    loss_z[z] = loss_own[...] + loss_other[...]
    to_z("loss_z", lambda z2: loss_z.at[z], loss_z.at[z], ssem_l, rsem_l.at[z], loss_z.at[pl.ds(0, 3)])
    for dz in range(1, 4):
        flying.add(f"loss_z{dz}", loss_z.at[(z + dz) & 3], rsem_l.at[(z + dz) & 3])
    for n in range(PARTS):
        flying.wait(f"e_cross{n}_in")
        whole_e = (half_e[:, span(n, WIDE)] + arrived_e[n].astype(f32)).astype(bf16)
        for g in range(4):
            fold_e[g, :, span(n, WIDE)] = whole_e[span(g, GROUP)]
    to_z("e", lambda z2: fold_e.at[z2], recv_e.at[z], ssem_e, rsem_e, fold_e.at[pl.ds(0, 3)])
    pltpu.make_async_copy(fold_e.at[z], recv_e.at[z], rsem_e).start()
    flying.add("e_in", recv_e, rsem_e)

    dact = jnp.zeros((16, H), f32)
    for n in range(PARTS):
        flying.wait(f"d{n}_in")
        unpack(sum_of(recv_d.at[n], 64), n)
        cols = span(n, WIDE)
        out_grad = x16[:, cols].astype(bf16)
        for s in range(OWN):
            dact = jnp.where(row_h == s, dact + nt(out_grad, reduce_[s, :, cols]), dact)
    dpre = (dact * gelu_slope).astype(bf16)
    dnormed = jnp.zeros((16, D), f32)
    for s in range(OWN):
        dnormed = jnp.where(row_d == s, nt(dpre, expand[s]), dnormed)
    normed_v = normed[...]
    dslot = (dnormed - normed_v * jnp.mean(dnormed * normed_v, axis=1, keepdims=True)) / root_mean
    msg_f[:, :Q] = (pack(dslot) / slot_total).astype(bf16)
    for dz in range(1, 4):
        flying.wait(f"loss_z{dz}")
    loss_line = ((loss_z[0] + loss_z[1]) + (loss_z[2] + loss_z[3]))[0:1, 0:1]
    loss_hi = loss_line.astype(bf16).astype(f32)
    loss_mid = (loss_line - loss_hi).astype(bf16).astype(f32)
    lane_f = lax.broadcasted_iota(jnp.int32, (16, LANES), 1)
    extra_f = jnp.where(lane_f == 0, best, 0.0)
    for n, value in enumerate((loss_hi, loss_mid, loss_line - loss_hi - loss_mid)):
        extra_f = jnp.where(lane_f == n + 1, value, extra_f)
    msg_f[:, Q:] = extra_f.astype(bf16)
    to_tok("f", lambda k: msg_f, recv_f, ssem_f, rsem_f)

    flying.wait("f_in")
    flying.wait("keys_z_out")
    for dz in range(4):
        flying.wait(f"keys_cross{dz}_out")
    back = nn(perm[...], recv_f[...].reshape(256, Q + LANES))
    for n in range(PARTS):
        for j in range(4):
            all_keys[0:GROUP, place(n, j)] = back[64 * j : 64 * j + 64, span(n)].astype(bf16)
    factor = jnp.exp(top - back[0:GROUP, Q : Q + 1])
    losses = jnp.sum(back[0:GROUP, Q + 1 : Q + 4], axis=(0, 1), keepdims=True) / OWN
    loss_o[...] = losses / (2.0 * TOK * ROWS * D)

    @pl.loop(0, ROWS // CHUNK)
    def _(n):
        at = pl.multiple_of(n * CHUNK, CHUNK)
        dprob = nt(all_keys[0:GROUP, :], tokens[pl.ds(at, CHUNK), :])
        weights[:, pl.ds(at, CHUNK)] = (terms[:, pl.ds(at, CHUNK)] * factor * dprob).astype(bf16)

    flying.wait("e_in")
    for n in range(PARTS):
        cols = span(n, WIDE)
        part = nn(weights[...], tokens[:, cols])
        for k in range(4):
            part += recv_e[k, :, cols].astype(f32)
        msg_g[n] = spread(lines(part)).reshape(TOK, 16, LANES)
        to_tok(f"g{n}", lambda k: msg_g.at[n, k], recv_g.at[n], ssem_g.at[n], rsem_g.at[n])
    for n in range(PARTS):
        flying.wait(f"g{n}_in")
        unpack(sum_of(recv_g.at[n], TOK) / D**0.5, n)
    grad_o[...] = x16[0:4, :]
    finish()


def hand_over(*refs):
    ins, outs, held, (sem_in, sem_out) = refs[:3], refs[3:6], refs[6:9], refs[9:]
    rows = [pl.ds(n * 112, 112) for n in range(4)]
    steps = [(ins[k], held[k], outs[k]) for k in (1, 2)]
    steps += [tuple(r.at[b] for r in (ins[0], held[0], outs[0])) for b in rows]
    first = [pltpu.make_async_copy(a, b, sem_in.at[n]) for n, (a, b, _) in enumerate(steps)]
    second = [pltpu.make_async_copy(b, c, sem_out.at[n]) for n, (_, b, c) in enumerate(steps)]
    for copy in first:
        copy.start()
    for n in range(len(steps)):
        first[n].wait()
        second[n].start()
    for copy in second:
        copy.wait()


def body(tokens, dispatch_keys, expand_weight, reduce_weight, teacher):
    any_spec = pl.BlockSpec(memory_space=pl.ANY)
    vmem_spec = pl.BlockSpec(memory_space=pltpu.VMEM)
    V = pltpu.VMEM
    dma = pltpu.SemaphoreType.DMA
    out_shape = (
        jax.ShapeDtypeStruct((PART, D), bf16),
        jax.ShapeDtypeStruct((1, 1), f32),
        jax.ShapeDtypeStruct((OWN, D), f32),
    )
    mixed, loss, grad = pl.pallas_call(
        kernel,
        out_shape=out_shape,
        in_specs=[any_spec, vmem_spec, any_spec, any_spec, any_spec],
        out_specs=(any_spec, vmem_spec, vmem_spec),
        scratch_shapes=[
            V((ROWS, D), bf16), V((OWN, D, H), bf16), V((OWN, H, D), bf16), V((PART, D), bf16),
            V((256, 256), bf16), V((256, 256), bf16), V((16, Q), f32),
            V((16, Q), bf16), V((TOK, 16, Q), bf16), V((2 * HALF, D), bf16),
            V((GROUP, ROWS), f32), V((GROUP, ROWS), bf16),
            V((PARTS + 1, TOK, 16, LANES), bf16), V((PARTS + 1, TOK, 16, LANES), bf16),
            V((16, D), f32), V((16, D), f32), V((PARTS, 16, LANES), bf16),
            V((PARTS, 2, 64, 16, LANES), bf16), V((2 * HALF, D), bf16),
            V((PART, 2 * HALF), f32), V((PART, 2 * HALF), bf16), V((PART, D), bf16), V((PART, D), bf16),
            V((HALF, D), f32), V((PARTS, HALF, WIDE), bf16), V((PARTS, HALF, WIDE), bf16),
            V((PARTS, 64, 16, LANES), bf16), V((PARTS, 64, 16, LANES), bf16),
            V((HALF, D), f32), V((PARTS, HALF, WIDE), bf16), V((PARTS, HALF, WIDE), bf16),
            V((4, GROUP, D), bf16), V((4, GROUP, D), bf16),
            V((8, LANES), f32), V((8, LANES), f32), V((4, 8, LANES), f32),
            V((16, Q + LANES), bf16), V((TOK, 16, Q + LANES), bf16),
            V((PARTS, TOK, 16, LANES), bf16), V((PARTS, TOK, 16, LANES), bf16),
            dma((4,)), dma, dma, dma, dma, dma((4,)), dma((4,)), dma((4,)),
            dma((PARTS + 1,)), dma((PARTS + 1,)), dma((PARTS,)), dma((PARTS,)), dma((PARTS,)), dma((PARTS,)),
            dma((PARTS,)), dma((PARTS,)), dma((PARTS,)), dma((PARTS,)), dma((PARTS,)), dma((PARTS,)), dma, dma,
            dma, dma, dma, dma((4,)), dma, dma, dma((PARTS,)), dma((PARTS,)),
        ],
        compiler_params=pltpu.CompilerParams(
            collective_id=0, has_side_effects=True, vmem_limit_bytes=56 * 2**20
        ),
    )(tokens, dispatch_keys, expand_weight, reduce_weight, teacher)
    mixed, loss, grad = pl.pallas_call(
        hand_over,
        out_shape=out_shape,
        in_specs=[any_spec] * 3,
        out_specs=(any_spec,) * 3,
        scratch_shapes=[V(o.shape, o.dtype) for o in out_shape] + [dma((6,)), dma((6,))],
    )(mixed, loss, grad)
    return mixed, loss.reshape(()), grad


def solution(mesh):
    in_specs = (
        P("tok", None),
        P(("tok", "exp"), None),
        P(("tok", "exp"), None, None),
        P(("tok", "exp"), None, None),
        P(("tok", "exp"), None),
    )
    out_specs = (P(("tok", "exp"), None), P(), P(("tok", "exp"), None))
    return jax.shard_map(body, mesh=mesh, in_specs=in_specs, out_specs=out_specs, check_vma=False)
```

```python
import functools
import jax
import jax.numpy as jnp
from jax import lax
from jax.experimental import pallas as pl
from jax.experimental.pallas import tpu as pltpu
from jax.sharding import PartitionSpec as P

MESH = pl.DeviceIdType.MESH
f32, bf16 = jnp.float32, jnp.bfloat16
D, H, ROWS, PART, OWN, GROUP, HALF = 1536, 512, 3584, 448, 4, 64, 256
TOK = 16
PARTS = 3
WIDE = 512
LANES = 128
Q = PARTS * LANES
CHUNK = 3584
gelu_coef = 0.7978845608028654
cube_coef = 0.044715


def gelu_pair(values):
    tanh_value = jnp.tanh(gelu_coef * (values + cube_coef * values * values * values))
    output = 0.5 * values * (1.0 + tanh_value)
    derivative = 0.5 * (1.0 + tanh_value) + 0.5 * values * (
        1.0 - tanh_value * tanh_value
    ) * gelu_coef * (1.0 + 3.0 * cube_coef * values * values)
    return (output, derivative)


def nn(a, b):
    return lax.dot_general(a, b, (((1,), (0,)), ((), ())), preferred_element_type=f32)


def nt(a, b):
    return lax.dot_general(a, b, (((1,), (1,)), ((), ())), preferred_element_type=f32)


def tn(a, b):
    return lax.dot_general(a, b, (((0,), (0,)), ((), ())), preferred_element_type=f32)


def wait_bytes(ref, sem):
    pltpu.make_async_copy(ref, ref, sem).wait()


class Pending:
    def __init__(self):
        self.open = {}

    def add(self, name, ref, sem):
        self.open[name] = (ref, sem)

    def wait(self, name):
        wait_bytes(*self.open.pop(name))

    def finish(self):
        for name in list(self.open):
            self.wait(name)


def kernel(
    tokens_h, keys, expand_h, reduce_h, teacher_h,
    mixed_h, loss_o, grad_o,
    tokens, expand, reduce_, teacher, perm, perm_t, wide,
    key_msg, recv_k, all_keys,
    terms, weights, msg_b, recv_b,
    normed, x16, out_msg, gath_o, every_out,
    comb, comb_b, grad_rows, mixed,
    half_d, cross_d, arrived_d, msg_d, recv_d,
    half_e, cross_e, arrived_e, fold_e, recv_e, loss_own, loss_other, loss_z,
    msg_f, recv_f, msg_g, recv_g,
    load_sem, mixed_sem, ssem_k, rsem_k, ssem_kz, rsem_kz, csend_k, crecv_k,
    ssem_b, rsem_b, ssem_o, rsem_o, csend_o, crecv_o,
    csend_d, crecv_d, ssem_d, rsem_d, csend_e, crecv_e, ssem_e, rsem_e,
    csend_l, crecv_l, ssem_l, rsem_l, ssem_f, rsem_f, ssem_g, rsem_g,
):
    t = lax.axis_index("tok")
    e = lax.axis_index("exp")
    x, y = t >> 2, t & 3
    z, c = e >> 1, e & 1
    other = (t, z * 2 + 1 - c)
    flying = Pending()
    finish = flying.finish

    def offset(d):
        return 2 - 2 * (d & 1) + ((d + (d >> 1)) & 1)

    def peer(k):
        t2 = ((x + offset((k >> 2) & 3)) & 3) * 4 + ((y + offset(k & 3)) & 3)
        return t2, (z + offset(k >> 4)) & 3

    def peer_tok(k):
        return peer(k + 48)[0]

    barrier = pltpu.get_barrier_semaphore()

    def greet(k, carry):
        t2, z2 = peer(k)
        pl.semaphore_signal(barrier, inc=1, device_id=(t2, z2 * 2 + c), device_id_type=MESH)
        return carry

    lax.fori_loop(0, 63, greet, 0, unroll=9)
    pl.semaphore_signal(barrier, inc=1, device_id=other, device_id_type=MESH)

    for n, (name, src, dst) in enumerate((
        ("tokens", tokens_h, tokens), ("expand", expand_h, expand),
        ("reduce", reduce_h, reduce_), ("teacher", teacher_h, teacher),
    )):
        pltpu.make_async_copy(src, dst, load_sem.at[n]).start()
        flying.add(name, dst, load_sem.at[n])

    row = lax.broadcasted_iota(jnp.int32, (256, 256), 0)
    col = lax.broadcasted_iota(jnp.int32, (256, 256), 1)

    def moved(r):
        return ((r >> 2) & 15) * 16 + (r >> 6) * 4 + (r & 3)

    perm[...] = jnp.where(col == moved(row), 1.0, 0.0).astype(bf16)
    perm_t[...] = jnp.where(row == moved(col), 1.0, 0.0).astype(bf16)

    def place(n, j):
        return slice(WIDE * n + LANES * j, WIDE * n + LANES * j + LANES)

    def span(n, width=LANES):
        return slice(width * n, width * n + width)

    def pack(value):
        for n in range(PARTS):
            for j in range(4):
                wide[4 * j : 4 * j + 4, span(n)] = value[0:4, place(n, j)]
        return wide[...]

    def unpack(message, n):
        wide[:, span(n)] = message
        for j in range(4):
            x16[0:4, place(n, j)] = wide[4 * j : 4 * j + 4, span(n)]

    def lines(value):
        return jnp.concatenate([value[:, span(j)] for j in range(4)], axis=0).astype(bf16)

    def spread(stacked):
        return nn(perm_t[...], stacked).astype(bf16)

    def remote(src, dst, send, recv, device):
        pltpu.make_async_remote_copy(
            src, dst, send, recv, device_id=device, device_id_type=MESH
        ).start()

    def cross(name, src, dst, send, recv):
        remote(src, dst, send, recv, other)
        flying.add(name + "_out", src, send)
        flying.add(name + "_in", dst, recv)

    def to_tok(name, src_of, recv_ref, send, recv):
        pltpu.make_async_copy(src_of(t), recv_ref.at[t], recv).start()

        def step(k, carry):
            t2 = peer_tok(k)
            remote(src_of(t2), recv_ref.at[t], send, recv, (t2, e))
            return carry

        lax.fori_loop(0, TOK - 1, step, 0, unroll=True)
        flying.add(name + "_out", recv_ref.at[pl.ds(0, TOK - 1)], send)
        flying.add(name + "_in", recv_ref, recv)

    def to_all(name, src_of, recv_ref, send, recv):
        me = z * TOK + t
        pltpu.make_async_copy(src_of(me), recv_ref.at[me], recv).start()

        def step(k, carry):
            t2, z2 = peer(k)
            remote(src_of(z2 * TOK + t2), recv_ref.at[me], send, recv, (t2, z2 * 2 + c))
            return carry

        lax.fori_loop(0, 63, step, 0, unroll=9)
        flying.add(name + "_out", recv_ref.at[pl.ds(0, 63)], send)
        flying.add(name + "_in", recv_ref, recv)

    def to_z(name, src_of, dst, send, recv, three):
        for dz in range(1, 4):
            z2 = (z + dz) & 3
            remote(src_of(z2), dst, send, recv, (t, z2 * 2 + c))
        flying.add(name + "_out", three, send)

    def sum_of(ref, count):
        return lax.fori_loop(
            0, count, lambda k, s: s + ref[k].astype(f32), jnp.zeros(ref.shape[1:], f32), unroll=8
        )

    x16[...] = jnp.zeros((16, D), f32)
    key_msg[...] = pack(keys[...].astype(f32)).astype(bf16)
    pl.semaphore_wait(barrier, 64)

    to_tok("keys", lambda k: key_msg, recv_k, ssem_k, rsem_k)
    flying.wait("keys_in")
    mine = pl.ds(pl.multiple_of(z * GROUP, GROUP), GROUP)
    moved_k = nn(perm[...], recv_k[...].reshape(256, Q)).astype(bf16)
    for n in range(PARTS):
        for j in range(4):
            all_keys[mine, place(n, j)] = moved_k[64 * j : 64 * j + 64, span(n)]

    def key_rows(half, dz):
        return pl.ds(pl.multiple_of(half * HALF + ((z + dz) & 3) * GROUP, GROUP), GROUP)

    def key_cross(dz):
        zz = (z + dz) & 3
        cross(
            f"keys_cross{dz}", all_keys.at[key_rows(0, dz)], all_keys.at[key_rows(1, dz)],
            csend_k.at[zz], crecv_k.at[zz],
        )

    to_z(
        "keys_z", lambda z2: all_keys.at[mine], all_keys.at[mine], ssem_kz, rsem_kz.at[z],
        all_keys.at[pl.ds(0, 3 * GROUP)],
    )
    for dz in range(1, 4):
        flying.add(f"keys_z{dz}", all_keys.at[key_rows(0, dz)], rsem_kz.at[(z + dz) & 3])
    key_cross(0)
    flying.wait("tokens")

    @pl.loop(0, ROWS // CHUNK)
    def _(n):
        at = pl.multiple_of(n * CHUNK, CHUNK)
        terms[:, pl.ds(at, CHUNK)] = nt(all_keys[mine, :], tokens[pl.ds(at, CHUNK), :])

    top = jnp.max(terms[...], axis=1, keepdims=True).astype(bf16).astype(f32)
    exp_terms = jnp.exp(terms[...] - top)
    terms[...] = exp_terms
    weights[...] = exp_terms.astype(bf16)
    total = jnp.sum(exp_terms, axis=1, keepdims=True)
    lane = lax.broadcasted_iota(jnp.int32, (GROUP, LANES), 1)
    total_hi = total.astype(bf16).astype(f32)
    extra = jnp.where(
        lane == 0, top, jnp.where(lane == 1, total_hi, jnp.where(lane == 2, total - total_hi, 0.0))
    )
    extra_b = extra.astype(bf16)
    msg_b[PARTS] = spread(jnp.concatenate([extra_b] * 4, axis=0)).reshape(TOK, 16, LANES)
    to_tok("b3", lambda k: msg_b.at[PARTS, k], recv_b.at[PARTS], ssem_b.at[PARTS], rsem_b.at[PARTS])
    for n in range(PARTS):
        part = nn(weights[...], tokens[:, span(n, WIDE)])
        msg_b[n] = spread(lines(part)).reshape(TOK, 16, LANES)
        to_tok(f"b{n}", lambda k: msg_b.at[n, k], recv_b.at[n], ssem_b.at[n], rsem_b.at[n])

    flying.wait("b3_in")
    best = recv_b[PARTS, 0, :, 0:1].astype(f32)
    for k in range(1, TOK):
        best = jnp.maximum(best, recv_b[PARTS, k, :, 0:1].astype(f32))
    scales = []
    slot_total = jnp.zeros((16, 1), f32)
    for k in range(TOK):
        held = recv_b[PARTS, k].astype(f32)
        scales.append(jnp.exp(held[:, 0:1] - best))
        slot_total += scales[k] * (held[:, 1:2] + held[:, 2:3])
    for n in range(PARTS):
        flying.wait(f"b{n}_in")
        slot_sum = jnp.zeros((16, LANES), f32)
        for k in range(TOK):
            slot_sum += scales[k] * recv_b[n, k].astype(f32)
        unpack(slot_sum / slot_total, n)
    slot_in = x16[...]
    root_mean = jnp.sqrt(jnp.mean(slot_in * slot_in, axis=1, keepdims=True) + 1e-06)
    normed_v = slot_in / root_mean
    normed[...] = normed_v
    normed_b = normed_v.astype(bf16)

    flying.wait("expand")
    flying.wait("reduce")
    row_h = lax.broadcasted_iota(jnp.int32, (16, H), 0)
    row_d = lax.broadcasted_iota(jnp.int32, (16, D), 0)
    pre_act = jnp.zeros((16, H), f32)
    for s in range(OWN):
        pre_act = jnp.where(row_h == s, nn(normed_b, expand[s]), pre_act)
    act_value, gelu_slope = gelu_pair(pre_act)
    act_b = act_value.astype(bf16)
    slot_out = jnp.zeros((16, D), f32)
    for s in range(OWN):
        slot_out = jnp.where(row_d == s, nn(act_b, reduce_[s]), slot_out)
    packed_out = pack(slot_out).astype(bf16)
    for n in range(PARTS):
        out_msg[n] = packed_out[:, span(n)]
    for n in range(PARTS):
        to_all(f"o{n}", lambda k: out_msg.at[n], gath_o.at[n, 0], ssem_o.at[n], rsem_o.at[n])

    for dz in range(1, 4):
        flying.wait(f"keys_z{dz}")
        key_cross(dz)
    for dz in range(4):
        flying.wait(f"keys_cross{dz}_in")
    local = tokens.at[pl.ds(pl.multiple_of(e * PART, GROUP), PART)]
    scores = nt(local[...], all_keys[...])
    row_terms = jnp.exp(scores - jnp.max(scores, axis=1, keepdims=True))
    comb_v = row_terms / jnp.sum(row_terms, axis=1, keepdims=True)
    comb[...] = comb_v
    comb_b[...] = comb_v.astype(bf16)

    flying.wait("teacher")

    def settle(n, half):
        block = jnp.concatenate(
            [gath_o[n, half, span(g, TOK)].reshape(256, LANES) for g in range(4)], axis=1
        )
        r = nn(perm[...], block).astype(bf16)
        for g in range(4):
            for j in range(4):
                every_out[half * HALF + g * GROUP : half * HALF + (g + 1) * GROUP, place(n, j)] = r[
                    64 * j : 64 * j + 64, span(g)
                ]

    def pass_on(n):
        flying.wait(f"o{n}_in")
        cross(f"o_cross{n}", gath_o.at[n, 0], gath_o.at[n, 1], csend_o.at[n], crecv_o.at[n])
        settle(n, 0)

    def combine(n):
        flying.wait(f"o_cross{n}_in")
        settle(n, 1)
        cols = span(n, WIDE)
        result = nn(comb_b[...], every_out[:, cols])
        mixed[:, cols] = result.astype(bf16)
        misfit = result - teacher[:, cols].astype(f32)
        grad_v = (misfit / D).astype(bf16)
        grad_rows[:, cols] = grad_v
        out_part = tn(comb_b[...], grad_v)
        half_d[:, cols] = out_part[:HALF]
        cross_d[n] = out_part[HALF:].astype(bf16)
        cross(f"d_cross{n}", cross_d.at[n], arrived_d.at[n], csend_d.at[n], crecv_d.at[n])
        return jnp.sum(misfit * misfit)

    def send_d(n):
        flying.wait(f"d_cross{n}_in")
        whole = half_d[:, span(n, WIDE)] + arrived_d[n].astype(f32)
        stacked = jnp.concatenate([lines(whole[span(g, GROUP)]) for g in range(4)], axis=1)
        r = spread(stacked)
        for g in range(4):
            msg_d[n, span(g, TOK)] = r[:, span(g)].reshape(TOK, 16, LANES)
        to_all(f"d{n}", lambda k: msg_d.at[n, k], recv_d.at[n], ssem_d.at[n], rsem_d.at[n])

    pass_on(0)
    loss_sum = combine(0)
    pass_on(1)
    send_d(0)
    loss_sum += combine(1)
    pass_on(2)
    send_d(1)
    loss_sum += combine(2)
    loss_own[...] = jnp.full((8, LANES), loss_sum, f32)
    cross("loss", loss_own, loss_other, csend_l, crecv_l)
    send_d(2)
    pltpu.make_async_copy(mixed, mixed_h, mixed_sem).start()
    flying.add("mixed", mixed, mixed_sem)

    dcomb = nt(grad_rows[...], every_out[...])
    weighted_d = comb[...] * dcomb
    dscore = (weighted_d - comb[...] * jnp.sum(weighted_d, axis=1, keepdims=True)).astype(bf16)
    for n in range(PARTS):
        key_part = tn(dscore, local[:, span(n, WIDE)])
        half_e[:, span(n, WIDE)] = key_part[:HALF]
        cross_e[n] = key_part[HALF:].astype(bf16)
        cross(f"e_cross{n}", cross_e.at[n], arrived_e.at[n], csend_e.at[n], crecv_e.at[n])
    flying.wait("loss_in")
    loss_z[z] = loss_own[...] + loss_other[...]
    to_z("loss_z", lambda z2: loss_z.at[z], loss_z.at[z], ssem_l, rsem_l.at[z], loss_z.at[pl.ds(0, 3)])
    for dz in range(1, 4):
        flying.add(f"loss_z{dz}", loss_z.at[(z + dz) & 3], rsem_l.at[(z + dz) & 3])
    for n in range(PARTS):
        flying.wait(f"e_cross{n}_in")
        whole_e = (half_e[:, span(n, WIDE)] + arrived_e[n].astype(f32)).astype(bf16)
        for g in range(4):
            fold_e[g, :, span(n, WIDE)] = whole_e[span(g, GROUP)]
    to_z("e", lambda z2: fold_e.at[z2], recv_e.at[z], ssem_e, rsem_e, fold_e.at[pl.ds(0, 3)])
    pltpu.make_async_copy(fold_e.at[z], recv_e.at[z], rsem_e).start()
    flying.add("e_in", recv_e, rsem_e)

    dact = jnp.zeros((16, H), f32)
    for n in range(PARTS):
        flying.wait(f"d{n}_in")
        unpack(sum_of(recv_d.at[n], 64), n)
        cols = span(n, WIDE)
        out_grad = x16[:, cols].astype(bf16)
        for s in range(OWN):
            dact = jnp.where(row_h == s, dact + nt(out_grad, reduce_[s, :, cols]), dact)
    dpre = (dact * gelu_slope).astype(bf16)
    dnormed = jnp.zeros((16, D), f32)
    for s in range(OWN):
        dnormed = jnp.where(row_d == s, nt(dpre, expand[s]), dnormed)
    normed_v = normed[...]
    dslot = (dnormed - normed_v * jnp.mean(dnormed * normed_v, axis=1, keepdims=True)) / root_mean
    msg_f[:, :Q] = (pack(dslot) / slot_total).astype(bf16)
    for dz in range(1, 4):
        flying.wait(f"loss_z{dz}")
    loss_line = ((loss_z[0] + loss_z[1]) + (loss_z[2] + loss_z[3]))[0:1, 0:1]
    loss_hi = loss_line.astype(bf16).astype(f32)
    loss_mid = (loss_line - loss_hi).astype(bf16).astype(f32)
    lane_f = lax.broadcasted_iota(jnp.int32, (16, LANES), 1)
    extra_f = jnp.where(lane_f == 0, best, 0.0)
    for n, value in enumerate((loss_hi, loss_mid, loss_line - loss_hi - loss_mid)):
        extra_f = jnp.where(lane_f == n + 1, value, extra_f)
    msg_f[:, Q:] = extra_f.astype(bf16)
    to_tok("f", lambda k: msg_f, recv_f, ssem_f, rsem_f)

    flying.wait("f_in")
    flying.wait("keys_z_out")
    for dz in range(4):
        flying.wait(f"keys_cross{dz}_out")
    back = nn(perm[...], recv_f[...].reshape(256, Q + LANES))
    for n in range(PARTS):
        for j in range(4):
            all_keys[0:GROUP, place(n, j)] = back[64 * j : 64 * j + 64, span(n)].astype(bf16)
    factor = jnp.exp(top - back[0:GROUP, Q : Q + 1])
    losses = jnp.sum(back[0:GROUP, Q + 1 : Q + 4], axis=(0, 1), keepdims=True) / OWN
    loss_o[...] = losses / (2.0 * TOK * ROWS * D)

    @pl.loop(0, ROWS // CHUNK)
    def _(n):
        at = pl.multiple_of(n * CHUNK, CHUNK)
        dprob = nt(all_keys[0:GROUP, :], tokens[pl.ds(at, CHUNK), :])
        weights[:, pl.ds(at, CHUNK)] = (terms[:, pl.ds(at, CHUNK)] * factor * dprob).astype(bf16)

    flying.wait("e_in")
    for n in range(PARTS):
        cols = span(n, WIDE)
        part = nn(weights[...], tokens[:, cols])
        for k in range(4):
            part += recv_e[k, :, cols].astype(f32)
        msg_g[n] = spread(lines(part)).reshape(TOK, 16, LANES)
        to_tok(f"g{n}", lambda k: msg_g.at[n, k], recv_g.at[n], ssem_g.at[n], rsem_g.at[n])
    for n in range(PARTS):
        flying.wait(f"g{n}_in")
        unpack(sum_of(recv_g.at[n], TOK) / D**0.5, n)
    grad_o[...] = x16[0:4, :]
    finish()


def hand_over(*refs):
    ins, outs, held, (sem_in, sem_out) = refs[:3], refs[3:6], refs[6:9], refs[9:]
    rows = [pl.ds(n * 112, 112) for n in range(4)]
    steps = [(ins[k], held[k], outs[k]) for k in (1, 2)]
    steps += [tuple(r.at[b] for r in (ins[0], held[0], outs[0])) for b in rows]
    first = [pltpu.make_async_copy(a, b, sem_in.at[n]) for n, (a, b, _) in enumerate(steps)]
    second = [pltpu.make_async_copy(b, c, sem_out.at[n]) for n, (_, b, c) in enumerate(steps)]
    for copy in first:
        copy.start()
    for n in range(len(steps)):
        first[n].wait()
        second[n].start()
    for copy in second:
        copy.wait()


def body(tokens, dispatch_keys, expand_weight, reduce_weight, teacher):
    any_spec = pl.BlockSpec(memory_space=pl.ANY)
    vmem_spec = pl.BlockSpec(memory_space=pltpu.VMEM)
    V = pltpu.VMEM
    dma = pltpu.SemaphoreType.DMA
    out_shape = (
        jax.ShapeDtypeStruct((PART, D), bf16),
        jax.ShapeDtypeStruct((1, 1), f32),
        jax.ShapeDtypeStruct((OWN, D), f32),
    )
    mixed, loss, grad = pl.pallas_call(
        kernel,
        out_shape=out_shape,
        in_specs=[any_spec, vmem_spec, any_spec, any_spec, any_spec],
        out_specs=(any_spec, vmem_spec, vmem_spec),
        scratch_shapes=[
            V((ROWS, D), bf16), V((OWN, D, H), bf16), V((OWN, H, D), bf16), V((PART, D), bf16),
            V((256, 256), bf16), V((256, 256), bf16), V((16, Q), f32),
            V((16, Q), bf16), V((TOK, 16, Q), bf16), V((2 * HALF, D), bf16),
            V((GROUP, ROWS), f32), V((GROUP, ROWS), bf16),
            V((PARTS + 1, TOK, 16, LANES), bf16), V((PARTS + 1, TOK, 16, LANES), bf16),
            V((16, D), f32), V((16, D), f32), V((PARTS, 16, LANES), bf16),
            V((PARTS, 2, 64, 16, LANES), bf16), V((2 * HALF, D), bf16),
            V((PART, 2 * HALF), f32), V((PART, 2 * HALF), bf16), V((PART, D), bf16), V((PART, D), bf16),
            V((HALF, D), f32), V((PARTS, HALF, WIDE), bf16), V((PARTS, HALF, WIDE), bf16),
            V((PARTS, 64, 16, LANES), bf16), V((PARTS, 64, 16, LANES), bf16),
            V((HALF, D), f32), V((PARTS, HALF, WIDE), bf16), V((PARTS, HALF, WIDE), bf16),
            V((4, GROUP, D), bf16), V((4, GROUP, D), bf16),
            V((8, LANES), f32), V((8, LANES), f32), V((4, 8, LANES), f32),
            V((16, Q + LANES), bf16), V((TOK, 16, Q + LANES), bf16),
            V((PARTS, TOK, 16, LANES), bf16), V((PARTS, TOK, 16, LANES), bf16),
            dma((4,)), dma, dma, dma, dma, dma((4,)), dma((4,)), dma((4,)),
            dma((PARTS + 1,)), dma((PARTS + 1,)), dma((PARTS,)), dma((PARTS,)), dma((PARTS,)), dma((PARTS,)),
            dma((PARTS,)), dma((PARTS,)), dma((PARTS,)), dma((PARTS,)), dma((PARTS,)), dma((PARTS,)), dma, dma,
            dma, dma, dma, dma((4,)), dma, dma, dma((PARTS,)), dma((PARTS,)),
        ],
        compiler_params=pltpu.CompilerParams(
            collective_id=0, has_side_effects=True, vmem_limit_bytes=56 * 2**20
        ),
    )(tokens, dispatch_keys, expand_weight, reduce_weight, teacher)
    mixed, loss, grad = pl.pallas_call(
        hand_over,
        out_shape=out_shape,
        in_specs=[any_spec] * 3,
        out_specs=(any_spec,) * 3,
        scratch_shapes=[V(o.shape, o.dtype) for o in out_shape] + [dma((6,)), dma((6,))],
    )(mixed, loss, grad)
    return mixed, loss.reshape(()), grad


def solution(mesh):
    in_specs = (
        P("tok", None),
        P(("tok", "exp"), None),
        P(("tok", "exp"), None, None),
        P(("tok", "exp"), None, None),
        P(("tok", "exp"), None),
    )
    out_specs = (P(("tok", "exp"), None), P(), P(("tok", "exp"), None))
    return jax.shard_map(body, mesh=mesh, in_specs=in_specs, out_specs=out_specs, check_vma=False)
```

```python
import functools
import jax
import jax.numpy as jnp
from jax import lax
from jax.experimental import pallas as pl
from jax.experimental.pallas import tpu as pltpu
from jax.sharding import PartitionSpec as P

MESH = pl.DeviceIdType.MESH
f32, bf16 = jnp.float32, jnp.bfloat16
D, H, ROWS, PART, OWN, GROUP, HALF = 1536, 512, 3584, 448, 4, 64, 256
TOK = 16
PARTS = 3
WIDE = 512
LANES = 128
Q = PARTS * LANES
CHUNK = 3584
gelu_coef = 0.7978845608028654
cube_coef = 0.044715


def gelu_pair(values):
    tanh_value = jnp.tanh(gelu_coef * (values + cube_coef * values * values * values))
    output = 0.5 * values * (1.0 + tanh_value)
    derivative = 0.5 * (1.0 + tanh_value) + 0.5 * values * (
        1.0 - tanh_value * tanh_value
    ) * gelu_coef * (1.0 + 3.0 * cube_coef * values * values)
    return (output, derivative)


def nn(a, b):
    return lax.dot_general(a, b, (((1,), (0,)), ((), ())), preferred_element_type=f32)


def nt(a, b):
    return lax.dot_general(a, b, (((1,), (1,)), ((), ())), preferred_element_type=f32)


def tn(a, b):
    return lax.dot_general(a, b, (((0,), (0,)), ((), ())), preferred_element_type=f32)


def wait_bytes(ref, sem):
    pltpu.make_async_copy(ref, ref, sem).wait()


class Pending:
    def __init__(self):
        self.open = {}

    def add(self, name, ref, sem):
        self.open[name] = (ref, sem)

    def wait(self, name):
        wait_bytes(*self.open.pop(name))

    def finish(self):
        for name in list(self.open):
            self.wait(name)


def kernel(
    tokens_h, keys, expand_h, reduce_h, teacher_h,
    mixed_h, loss_o, grad_o,
    tokens, expand, reduce_, teacher, perm, perm_t, wide,
    key_msg, recv_k, all_keys,
    terms, weights, msg_b, recv_b,
    normed, x16, out_msg, gath_o, every_out,
    comb, comb_b, grad_rows, mixed,
    half_d, cross_d, arrived_d, msg_d, recv_d,
    half_e, cross_e, arrived_e, fold_e, recv_e, loss_own, loss_other, loss_z,
    msg_f, recv_f, msg_g, recv_g,
    load_sem, mixed_sem, ssem_k, rsem_k, ssem_kz, rsem_kz, csend_k, crecv_k,
    ssem_b, rsem_b, ssem_o, rsem_o, csend_o, crecv_o,
    csend_d, crecv_d, ssem_d, rsem_d, csend_e, crecv_e, ssem_e, rsem_e,
    csend_l, crecv_l, ssem_l, rsem_l, ssem_f, rsem_f, ssem_g, rsem_g,
):
    t = lax.axis_index("tok")
    e = lax.axis_index("exp")
    x, y = t >> 2, t & 3
    z, c = e >> 1, e & 1
    other = (t, z * 2 + 1 - c)
    flying = Pending()
    finish = flying.finish

    def offset(d):
        return 2 - 2 * (d & 1) + ((d + (d >> 1)) & 1)

    def peer(k):
        t2 = ((x + offset((k >> 2) & 3)) & 3) * 4 + ((y + offset(k & 3)) & 3)
        return t2, (z + offset(k >> 4)) & 3

    def peer_tok(k):
        return peer(k + 48)[0]

    barrier = pltpu.get_barrier_semaphore()

    def greet(k, carry):
        t2, z2 = peer(k)
        pl.semaphore_signal(barrier, inc=1, device_id=(t2, z2 * 2 + c), device_id_type=MESH)
        return carry

    lax.fori_loop(0, 63, greet, 0, unroll=9)
    pl.semaphore_signal(barrier, inc=1, device_id=other, device_id_type=MESH)

    for n, (name, src, dst) in enumerate((
        ("tokens", tokens_h, tokens), ("expand", expand_h, expand),
        ("reduce", reduce_h, reduce_), ("teacher", teacher_h, teacher),
    )):
        pltpu.make_async_copy(src, dst, load_sem.at[n]).start()
        flying.add(name, dst, load_sem.at[n])

    row = lax.broadcasted_iota(jnp.int32, (256, 256), 0)
    col = lax.broadcasted_iota(jnp.int32, (256, 256), 1)

    def moved(r):
        return ((r >> 2) & 15) * 16 + (r >> 6) * 4 + (r & 3)

    perm[...] = jnp.where(col == moved(row), 1.0, 0.0).astype(bf16)
    perm_t[...] = jnp.where(row == moved(col), 1.0, 0.0).astype(bf16)

    def place(n, j):
        return slice(WIDE * n + LANES * j, WIDE * n + LANES * j + LANES)

    def span(n, width=LANES):
        return slice(width * n, width * n + width)

    def pack(value):
        for n in range(PARTS):
            for j in range(4):
                wide[4 * j : 4 * j + 4, span(n)] = value[0:4, place(n, j)]
        return wide[...]

    def unpack(message, n):
        wide[:, span(n)] = message
        for j in range(4):
            x16[0:4, place(n, j)] = wide[4 * j : 4 * j + 4, span(n)]

    def lines(value):
        return jnp.concatenate([value[:, span(j)] for j in range(4)], axis=0).astype(bf16)

    def spread(stacked):
        return nn(perm_t[...], stacked).astype(bf16)

    def remote(src, dst, send, recv, device):
        pltpu.make_async_remote_copy(
            src, dst, send, recv, device_id=device, device_id_type=MESH
        ).start()

    def cross(name, src, dst, send, recv):
        remote(src, dst, send, recv, other)
        flying.add(name + "_out", src, send)
        flying.add(name + "_in", dst, recv)

    def to_tok(name, src_of, recv_ref, send, recv):
        pltpu.make_async_copy(src_of(t), recv_ref.at[t], recv).start()

        def step(k, carry):
            t2 = peer_tok(k)
            remote(src_of(t2), recv_ref.at[t], send, recv, (t2, e))
            return carry

        lax.fori_loop(0, TOK - 1, step, 0, unroll=True)
        flying.add(name + "_out", recv_ref.at[pl.ds(0, TOK - 1)], send)
        flying.add(name + "_in", recv_ref, recv)

    def to_all(name, src_of, recv_ref, send, recv):
        me = z * TOK + t
        pltpu.make_async_copy(src_of(me), recv_ref.at[me], recv).start()

        def step(k, carry):
            t2, z2 = peer(k)
            remote(src_of(z2 * TOK + t2), recv_ref.at[me], send, recv, (t2, z2 * 2 + c))
            return carry

        lax.fori_loop(0, 63, step, 0, unroll=9)
        flying.add(name + "_out", recv_ref.at[pl.ds(0, 63)], send)
        flying.add(name + "_in", recv_ref, recv)

    def to_z(name, src_of, dst, send, recv, three):
        for dz in range(1, 4):
            z2 = (z + dz) & 3
            remote(src_of(z2), dst, send, recv, (t, z2 * 2 + c))
        flying.add(name + "_out", three, send)

    def sum_of(ref, count):
        return lax.fori_loop(
            0, count, lambda k, s: s + ref[k].astype(f32), jnp.zeros(ref.shape[1:], f32), unroll=8
        )

    x16[...] = jnp.zeros((16, D), f32)
    key_msg[...] = pack(keys[...].astype(f32)).astype(bf16)
    pl.semaphore_wait(barrier, 64)

    to_tok("keys", lambda k: key_msg, recv_k, ssem_k, rsem_k)
    flying.wait("keys_in")
    mine = pl.ds(pl.multiple_of(z * GROUP, GROUP), GROUP)
    moved_k = nn(perm[...], recv_k[...].reshape(256, Q)).astype(bf16)
    for n in range(PARTS):
        for j in range(4):
            all_keys[mine, place(n, j)] = moved_k[64 * j : 64 * j + 64, span(n)]

    def key_rows(half, dz):
        return pl.ds(pl.multiple_of(half * HALF + ((z + dz) & 3) * GROUP, GROUP), GROUP)

    def key_cross(dz):
        zz = (z + dz) & 3
        cross(
            f"keys_cross{dz}", all_keys.at[key_rows(0, dz)], all_keys.at[key_rows(1, dz)],
            csend_k.at[zz], crecv_k.at[zz],
        )

    to_z(
        "keys_z", lambda z2: all_keys.at[mine], all_keys.at[mine], ssem_kz, rsem_kz.at[z],
        all_keys.at[pl.ds(0, 3 * GROUP)],
    )
    for dz in range(1, 4):
        flying.add(f"keys_z{dz}", all_keys.at[key_rows(0, dz)], rsem_kz.at[(z + dz) & 3])
    key_cross(0)
    flying.wait("tokens")

    @pl.loop(0, ROWS // CHUNK)
    def _(n):
        at = pl.multiple_of(n * CHUNK, CHUNK)
        terms[:, pl.ds(at, CHUNK)] = nt(all_keys[mine, :], tokens[pl.ds(at, CHUNK), :])

    top = jnp.max(terms[...], axis=1, keepdims=True).astype(bf16).astype(f32)
    exp_terms = jnp.exp(terms[...] - top)
    terms[...] = exp_terms
    weights[...] = exp_terms.astype(bf16)
    total = jnp.sum(exp_terms, axis=1, keepdims=True)
    lane = lax.broadcasted_iota(jnp.int32, (GROUP, LANES), 1)
    total_hi = total.astype(bf16).astype(f32)
    extra = jnp.where(
        lane == 0, top, jnp.where(lane == 1, total_hi, jnp.where(lane == 2, total - total_hi, 0.0))
    )
    extra_b = extra.astype(bf16)
    msg_b[PARTS] = spread(jnp.concatenate([extra_b] * 4, axis=0)).reshape(TOK, 16, LANES)
    to_tok("b3", lambda k: msg_b.at[PARTS, k], recv_b.at[PARTS], ssem_b.at[PARTS], rsem_b.at[PARTS])
    for n in range(PARTS):
        part = nn(weights[...], tokens[:, span(n, WIDE)])
        msg_b[n] = spread(lines(part)).reshape(TOK, 16, LANES)
        to_tok(f"b{n}", lambda k: msg_b.at[n, k], recv_b.at[n], ssem_b.at[n], rsem_b.at[n])

    flying.wait("b3_in")
    best = recv_b[PARTS, 0, :, 0:1].astype(f32)
    for k in range(1, TOK):
        best = jnp.maximum(best, recv_b[PARTS, k, :, 0:1].astype(f32))
    scales = []
    slot_total = jnp.zeros((16, 1), f32)
    for k in range(TOK):
        held = recv_b[PARTS, k].astype(f32)
        scales.append(jnp.exp(held[:, 0:1] - best))
        slot_total += scales[k] * (held[:, 1:2] + held[:, 2:3])
    for n in range(PARTS):
        flying.wait(f"b{n}_in")
        slot_sum = jnp.zeros((16, LANES), f32)
        for k in range(TOK):
            slot_sum += scales[k] * recv_b[n, k].astype(f32)
        unpack(slot_sum / slot_total, n)
    slot_in = x16[...]
    root_mean = jnp.sqrt(jnp.mean(slot_in * slot_in, axis=1, keepdims=True) + 1e-06)
    normed_v = slot_in / root_mean
    normed[...] = normed_v
    normed_b = normed_v.astype(bf16)

    flying.wait("expand")
    flying.wait("reduce")
    row_h = lax.broadcasted_iota(jnp.int32, (16, H), 0)
    row_d = lax.broadcasted_iota(jnp.int32, (16, D), 0)
    pre_act = jnp.zeros((16, H), f32)
    for s in range(OWN):
        pre_act = jnp.where(row_h == s, nn(normed_b, expand[s]), pre_act)
    act_value, gelu_slope = gelu_pair(pre_act)
    act_b = act_value.astype(bf16)
    slot_out = jnp.zeros((16, D), f32)
    for s in range(OWN):
        slot_out = jnp.where(row_d == s, nn(act_b, reduce_[s]), slot_out)
    packed_out = pack(slot_out).astype(bf16)
    for n in range(PARTS):
        out_msg[n] = packed_out[:, span(n)]
    for n in range(PARTS):
        to_all(f"o{n}", lambda k: out_msg.at[n], gath_o.at[n, 0], ssem_o.at[n], rsem_o.at[n])

    for dz in range(1, 4):
        flying.wait(f"keys_z{dz}")
        key_cross(dz)
    for dz in range(4):
        flying.wait(f"keys_cross{dz}_in")
    local = tokens.at[pl.ds(pl.multiple_of(e * PART, GROUP), PART)]
    scores = nt(local[...], all_keys[...])
    row_terms = jnp.exp(scores - jnp.max(scores, axis=1, keepdims=True))
    comb_v = row_terms / jnp.sum(row_terms, axis=1, keepdims=True)
    comb[...] = comb_v
    comb_b[...] = comb_v.astype(bf16)

    flying.wait("teacher")

    def settle(n, half):
        block = jnp.concatenate(
            [gath_o[n, half, span(g, TOK)].reshape(256, LANES) for g in range(4)], axis=1
        )
        r = nn(perm[...], block).astype(bf16)
        for g in range(4):
            for j in range(4):
                every_out[half * HALF + g * GROUP : half * HALF + (g + 1) * GROUP, place(n, j)] = r[
                    64 * j : 64 * j + 64, span(g)
                ]

    def pass_on(n):
        flying.wait(f"o{n}_in")
        cross(f"o_cross{n}", gath_o.at[n, 0], gath_o.at[n, 1], csend_o.at[n], crecv_o.at[n])
        settle(n, 0)

    def combine(n):
        flying.wait(f"o_cross{n}_in")
        settle(n, 1)
        cols = span(n, WIDE)
        result = nn(comb_b[...], every_out[:, cols])
        mixed[:, cols] = result.astype(bf16)
        misfit = result - teacher[:, cols].astype(f32)
        grad_v = (misfit / D).astype(bf16)
        grad_rows[:, cols] = grad_v
        out_part = tn(comb_b[...], grad_v)
        half_d[:, cols] = out_part[:HALF]
        cross_d[n] = out_part[HALF:].astype(bf16)
        cross(f"d_cross{n}", cross_d.at[n], arrived_d.at[n], csend_d.at[n], crecv_d.at[n])
        return jnp.sum(misfit * misfit)

    def send_d(n):
        flying.wait(f"d_cross{n}_in")
        whole = half_d[:, span(n, WIDE)] + arrived_d[n].astype(f32)
        stacked = jnp.concatenate([lines(whole[span(g, GROUP)]) for g in range(4)], axis=1)
        r = spread(stacked)
        for g in range(4):
            msg_d[n, span(g, TOK)] = r[:, span(g)].reshape(TOK, 16, LANES)
        to_all(f"d{n}", lambda k: msg_d.at[n, k], recv_d.at[n], ssem_d.at[n], rsem_d.at[n])

    pass_on(0)
    loss_sum = combine(0)
    pass_on(1)
    send_d(0)
    loss_sum += combine(1)
    pass_on(2)
    send_d(1)
    loss_sum += combine(2)
    loss_own[...] = jnp.full((8, LANES), loss_sum, f32)
    cross("loss", loss_own, loss_other, csend_l, crecv_l)
    send_d(2)
    pltpu.make_async_copy(mixed, mixed_h, mixed_sem).start()
    flying.add("mixed", mixed, mixed_sem)

    dcomb = nt(grad_rows[...], every_out[...])
    weighted_d = comb[...] * dcomb
    dscore = (weighted_d - comb[...] * jnp.sum(weighted_d, axis=1, keepdims=True)).astype(bf16)
    for n in range(PARTS):
        key_part = tn(dscore, local[:, span(n, WIDE)])
        half_e[:, span(n, WIDE)] = key_part[:HALF]
        cross_e[n] = key_part[HALF:].astype(bf16)
        cross(f"e_cross{n}", cross_e.at[n], arrived_e.at[n], csend_e.at[n], crecv_e.at[n])
    flying.wait("loss_in")
    loss_z[z] = loss_own[...] + loss_other[...]
    to_z("loss_z", lambda z2: loss_z.at[z], loss_z.at[z], ssem_l, rsem_l.at[z], loss_z.at[pl.ds(0, 3)])
    for dz in range(1, 4):
        flying.add(f"loss_z{dz}", loss_z.at[(z + dz) & 3], rsem_l.at[(z + dz) & 3])
    for n in range(PARTS):
        flying.wait(f"e_cross{n}_in")
        whole_e = (half_e[:, span(n, WIDE)] + arrived_e[n].astype(f32)).astype(bf16)
        for g in range(4):
            fold_e[g, :, span(n, WIDE)] = whole_e[span(g, GROUP)]
    to_z("e", lambda z2: fold_e.at[z2], recv_e.at[z], ssem_e, rsem_e, fold_e.at[pl.ds(0, 3)])
    pltpu.make_async_copy(fold_e.at[z], recv_e.at[z], rsem_e).start()
    flying.add("e_in", recv_e, rsem_e)

    dact = jnp.zeros((16, H), f32)
    for n in range(PARTS):
        flying.wait(f"d{n}_in")
        unpack(sum_of(recv_d.at[n], 64), n)
        cols = span(n, WIDE)
        out_grad = x16[:, cols].astype(bf16)
        for s in range(OWN):
            dact = jnp.where(row_h == s, dact + nt(out_grad, reduce_[s, :, cols]), dact)
    dpre = (dact * gelu_slope).astype(bf16)
    dnormed = jnp.zeros((16, D), f32)
    for s in range(OWN):
        dnormed = jnp.where(row_d == s, nt(dpre, expand[s]), dnormed)
    normed_v = normed[...]
    dslot = (dnormed - normed_v * jnp.mean(dnormed * normed_v, axis=1, keepdims=True)) / root_mean
    msg_f[:, :Q] = (pack(dslot) / slot_total).astype(bf16)
    for dz in range(1, 4):
        flying.wait(f"loss_z{dz}")
    loss_line = ((loss_z[0] + loss_z[1]) + (loss_z[2] + loss_z[3]))[0:1, 0:1]
    loss_hi = loss_line.astype(bf16).astype(f32)
    loss_mid = (loss_line - loss_hi).astype(bf16).astype(f32)
    lane_f = lax.broadcasted_iota(jnp.int32, (16, LANES), 1)
    extra_f = jnp.where(lane_f == 0, best, 0.0)
    for n, value in enumerate((loss_hi, loss_mid, loss_line - loss_hi - loss_mid)):
        extra_f = jnp.where(lane_f == n + 1, value, extra_f)
    msg_f[:, Q:] = extra_f.astype(bf16)
    to_tok("f", lambda k: msg_f, recv_f, ssem_f, rsem_f)

    flying.wait("f_in")
    flying.wait("keys_z_out")
    for dz in range(4):
        flying.wait(f"keys_cross{dz}_out")
    back = nn(perm[...], recv_f[...].reshape(256, Q + LANES))
    for n in range(PARTS):
        for j in range(4):
            all_keys[0:GROUP, place(n, j)] = back[64 * j : 64 * j + 64, span(n)].astype(bf16)
    factor = jnp.exp(top - back[0:GROUP, Q : Q + 1])
    losses = jnp.sum(back[0:GROUP, Q + 1 : Q + 4], axis=(0, 1), keepdims=True) / OWN
    loss_o[...] = losses / (2.0 * TOK * ROWS * D)

    @pl.loop(0, ROWS // CHUNK)
    def _(n):
        at = pl.multiple_of(n * CHUNK, CHUNK)
        dprob = nt(all_keys[0:GROUP, :], tokens[pl.ds(at, CHUNK), :])
        weights[:, pl.ds(at, CHUNK)] = (terms[:, pl.ds(at, CHUNK)] * factor * dprob).astype(bf16)

    for n in range(PARTS):
        cols = span(n, WIDE)
        part = nn(weights[...], tokens[:, cols])
        if n == 0:
            flying.wait("e_in")
        for k in range(4):
            part += recv_e[k, :, cols].astype(f32)
        msg_g[n] = spread(lines(part)).reshape(TOK, 16, LANES)
        to_tok(f"g{n}", lambda k: msg_g.at[n, k], recv_g.at[n], ssem_g.at[n], rsem_g.at[n])
    for n in range(PARTS):
        flying.wait(f"g{n}_in")
        unpack(sum_of(recv_g.at[n], TOK) / D**0.5, n)
    grad_o[...] = x16[0:4, :]
    finish()


def hand_over(*refs):
    ins, outs, held, (sem_in, sem_out) = refs[:3], refs[3:6], refs[6:9], refs[9:]
    rows = [pl.ds(n * 112, 112) for n in range(4)]
    steps = [(ins[k], held[k], outs[k]) for k in (1, 2)]
    steps += [tuple(r.at[b] for r in (ins[0], held[0], outs[0])) for b in rows]
    first = [pltpu.make_async_copy(a, b, sem_in.at[n]) for n, (a, b, _) in enumerate(steps)]
    second = [pltpu.make_async_copy(b, c, sem_out.at[n]) for n, (_, b, c) in enumerate(steps)]
    for copy in first:
        copy.start()
    for n in range(len(steps)):
        first[n].wait()
        second[n].start()
    for copy in second:
        copy.wait()


def body(tokens, dispatch_keys, expand_weight, reduce_weight, teacher):
    any_spec = pl.BlockSpec(memory_space=pl.ANY)
    vmem_spec = pl.BlockSpec(memory_space=pltpu.VMEM)
    V = pltpu.VMEM
    dma = pltpu.SemaphoreType.DMA
    out_shape = (
        jax.ShapeDtypeStruct((PART, D), bf16),
        jax.ShapeDtypeStruct((1, 1), f32),
        jax.ShapeDtypeStruct((OWN, D), f32),
    )
    mixed, loss, grad = pl.pallas_call(
        kernel,
        out_shape=out_shape,
        in_specs=[any_spec, vmem_spec, any_spec, any_spec, any_spec],
        out_specs=(any_spec, vmem_spec, vmem_spec),
        scratch_shapes=[
            V((ROWS, D), bf16), V((OWN, D, H), bf16), V((OWN, H, D), bf16), V((PART, D), bf16),
            V((256, 256), bf16), V((256, 256), bf16), V((16, Q), f32),
            V((16, Q), bf16), V((TOK, 16, Q), bf16), V((2 * HALF, D), bf16),
            V((GROUP, ROWS), f32), V((GROUP, ROWS), bf16),
            V((PARTS + 1, TOK, 16, LANES), bf16), V((PARTS + 1, TOK, 16, LANES), bf16),
            V((16, D), f32), V((16, D), f32), V((PARTS, 16, LANES), bf16),
            V((PARTS, 2, 64, 16, LANES), bf16), V((2 * HALF, D), bf16),
            V((PART, 2 * HALF), f32), V((PART, 2 * HALF), bf16), V((PART, D), bf16), V((PART, D), bf16),
            V((HALF, D), f32), V((PARTS, HALF, WIDE), bf16), V((PARTS, HALF, WIDE), bf16),
            V((PARTS, 64, 16, LANES), bf16), V((PARTS, 64, 16, LANES), bf16),
            V((HALF, D), f32), V((PARTS, HALF, WIDE), bf16), V((PARTS, HALF, WIDE), bf16),
            V((4, GROUP, D), bf16), V((4, GROUP, D), bf16),
            V((8, LANES), f32), V((8, LANES), f32), V((4, 8, LANES), f32),
            V((16, Q + LANES), bf16), V((TOK, 16, Q + LANES), bf16),
            V((PARTS, TOK, 16, LANES), bf16), V((PARTS, TOK, 16, LANES), bf16),
            dma((4,)), dma, dma, dma, dma, dma((4,)), dma((4,)), dma((4,)),
            dma((PARTS + 1,)), dma((PARTS + 1,)), dma((PARTS,)), dma((PARTS,)), dma((PARTS,)), dma((PARTS,)),
            dma((PARTS,)), dma((PARTS,)), dma((PARTS,)), dma((PARTS,)), dma((PARTS,)), dma((PARTS,)), dma, dma,
            dma, dma, dma, dma((4,)), dma, dma, dma((PARTS,)), dma((PARTS,)),
        ],
        compiler_params=pltpu.CompilerParams(
            collective_id=0, has_side_effects=True, vmem_limit_bytes=56 * 2**20
        ),
    )(tokens, dispatch_keys, expand_weight, reduce_weight, teacher)
    mixed, loss, grad = pl.pallas_call(
        hand_over,
        out_shape=out_shape,
        in_specs=[any_spec] * 3,
        out_specs=(any_spec,) * 3,
        scratch_shapes=[V(o.shape, o.dtype) for o in out_shape] + [dma((6,)), dma((6,))],
    )(mixed, loss, grad)
    return mixed, loss.reshape(()), grad


def solution(mesh):
    in_specs = (
        P("tok", None),
        P(("tok", "exp"), None),
        P(("tok", "exp"), None, None),
        P(("tok", "exp"), None, None),
        P(("tok", "exp"), None),
    )
    out_specs = (P(("tok", "exp"), None), P(), P(("tok", "exp"), None))
    return jax.shard_map(body, mesh=mesh, in_specs=in_specs, out_specs=out_specs, check_vma=False)
```
